256 devices in a mesh: tm: 4 (over x), space: 64 (over z, y, core).
Axes of the slice: x: 4, y: 4, z: 8, core: 2. Of those that a mesh axis runs over, the one named last changes fastest.
Arguments:
- embeddings: bfloat16 [8, 131072, 128], P('tm', 'space'), may hold values from -8 to 8
- class_blocks: int32 [4, 64, 19, 8], P('tm', 'space'), may hold values from 0 to 31, as said below
- class_counts: int32 [4, 64, 19], P('tm', 'space'), may hold values from 0 to 8, as said below
- means: float32 [19, 5, 128], replicated, may hold values from -3 to 3
- log_weights: float32 [19, 5], replicated, may hold values from -21 to 1
- factors: bfloat16 [19, 5, 128, 128], replicated, may hold values from -1 to 4, as said below
Outputs:
- new_log_weights: float32 [19, 5], replicated
- new_means: float32 [19, 5, 128], replicated
- new_factors: float32 [19, 5, 128, 128], replicated
The draws below stay inside these ranges and needn't reach their ends.
Inputs may be any that keep to these rules, and one draw needn't show every extreme that they name: `class_blocks`: on each device, every class list names distinct local blocks and no block is named in two lists; entries beyond a list's count are arbitrary block indices. `class_counts`: on every device one class has exactly 8 blocks; on one device every block belongs to some class. `factors`: each factor is upper triangular with a positive diagonal.
All inputs are finite; a program needn't handle non-finite values.
Results may differ from the reference program's by a relative error of at most 0.0003.
Values sent between devices are 32-bit elements; how exact they have to be, the bound alone decides.
No kernel may reach another device: no remote copies, remote signals or barrier semaphores. Data moves between devices by JAX's collectives and lax.ppermute only.
A program may use at most 192 MiB of HBM per device.

```python
import math
import jax
import jax.numpy as jnp
from jax import lax

C = 19
K = 5
D = 128
BLOCK = 128
FR_DEV = 2
PIX_DEV = 2048
NBLK = 32
CAP = 8
N_TM = 4
N_SPACE = 64


def lists_and_counts(key):
    device_total = N_TM * N_SPACE
    device_keys = jax.random.split(key, device_total)

    def one_device(device_key, device_id):
        perm_key, major_key, valid_key, shift_key, filler_key = jax.random.split(device_key, 5)
        order = jax.random.permutation(perm_key, NBLK).astype(jnp.int32)
        major = jax.random.randint(major_key, (), 0, C, dtype=jnp.int32)
        valid_total = jnp.where(device_id == 0, NBLK, jax.random.randint(valid_key, (), CAP, NBLK + 1, dtype=jnp.int32))
        slot_ids = jnp.arange(NBLK, dtype=jnp.int32)
        shifts = jax.random.randint(shift_key, (NBLK,), 0, 2, dtype=jnp.int32)
        others = (major + 1 + (slot_ids - CAP + shifts) % (C - 1)) % C
        slot_class = jnp.where(slot_ids < CAP, major, others)
        live_slot = slot_ids < valid_total
        class_ids = jnp.arange(C, dtype=jnp.int32)
        member = (slot_class[None, :] == class_ids[:, None]) & live_slot[None, :]
        ranks = jnp.cumsum(member.astype(jnp.int32), axis=1) - 1
        columns = jnp.where(member, ranks, CAP)
        row_index = jnp.broadcast_to(class_ids[:, None], (C, NBLK))
        filler = jax.random.randint(filler_key, (C, CAP), 0, NBLK, dtype=jnp.int32)
        listed = filler.at[row_index, columns].set(jnp.broadcast_to(order[None, :], (C, NBLK)), mode='drop')
        return (listed, jnp.sum(member.astype(jnp.int32), axis=1))
    listed, list_counts = jax.vmap(one_device)(device_keys, jnp.arange(device_total, dtype=jnp.int32))
    return (listed.reshape(N_TM, N_SPACE, C, CAP), list_counts.reshape(N_TM, N_SPACE, C))


def draw_class_blocks(key, part):
    return lists_and_counts(key)[0]


def draw_class_counts(key, part):
    return lists_and_counts(key)[1]


def draw_embeddings(key, part):
    key = jax.random.fold_in(key, 11)
    base_key, scale_key, shift_key = jax.random.split(key, 3)
    shape_full = (FR_DEV * N_TM, N_SPACE, PIX_DEV, D)
    shape_group = (FR_DEV * N_TM, N_SPACE, 1, D)
    base_draw = jax.random.normal(base_key, shape_full, jnp.float32)
    spread = jnp.exp(jax.random.uniform(scale_key, shape_group, jnp.float32, math.log(0.5), math.log(2.0)))
    offset = 0.5 * jax.random.normal(shift_key, shape_group, jnp.float32)
    values = jnp.clip(base_draw * spread + offset, -8.0, 8.0)
    return values.reshape(FR_DEV * N_TM, N_SPACE * PIX_DEV, D).astype(jnp.bfloat16)


def draw_means(key, part):
    key = jax.random.fold_in(key, 31)
    mean_key = jax.random.fold_in(key, 0)
    values = jnp.clip(0.5 * jax.random.normal(mean_key, (C, K, D), jnp.float32), -3.0, 3.0)
    return values


def draw_log_weights(key, part):
    key = jax.random.fold_in(key, 37)
    weight_key = jax.random.fold_in(key, 0)
    base_draw = jax.random.uniform(weight_key, (C, K), jnp.float32, -1.0, 1.0)
    values = base_draw
    return values


def draw_factors(key, part):
    key = jax.random.fold_in(key, 23)
    diag_key, off_key = jax.random.split(key, 2)
    upper_mask = jnp.triu(jnp.ones((D, D), jnp.float32), 1)
    identity = jnp.eye(D, dtype=jnp.float32)
    off_part = jnp.clip(jax.random.normal(off_key, (C, K, D, D), jnp.float32), -2.5, 2.5) * (0.4 / math.sqrt(D))
    diagonal = jnp.exp(jax.random.uniform(diag_key, (C, K, D), jnp.float32, math.log(0.6), math.log(1.6)))
    values = off_part * upper_mask + diagonal[..., None] * identity
    return values.astype(jnp.bfloat16)


def setup_inputs(seed: int = 0) -> dict:
    arg_keys = jax.random.split(jax.random.key(seed), 7)
    embeddings = draw_embeddings(jax.random.fold_in(arg_keys[6], 71), 0)
    class_blocks = draw_class_blocks(jax.random.fold_in(arg_keys[6], 71), 0)
    class_counts = draw_class_counts(jax.random.fold_in(arg_keys[6], 71), 0)
    means = draw_means(jax.random.fold_in(arg_keys[6], 71), 0)
    log_weights = draw_log_weights(jax.random.fold_in(arg_keys[6], 71), 0)
    factors = draw_factors(jax.random.fold_in(arg_keys[6], 71), 0)
    return {"embeddings": embeddings, "class_blocks": class_blocks, "class_counts": class_counts, "means": means, "log_weights": log_weights, "factors": factors}


prior_weight = 1.0
prior_spread = 1.0
highest = lax.Precision.HIGHEST

def block_stats(block_rows, block_class, block_live, factors, mean_proj, log_const):
    gathered = factors[block_class].astype(jnp.float32)
    rows_float = block_rows.astype(jnp.float32)
    projected = jnp.einsum('bpi,bkij->bpkj', rows_float, gathered, precision=highest)
    centred = projected - mean_proj[block_class][:, None, :, :]
    scores = log_const[block_class][:, None, :] - 0.5 * jnp.sum(centred * centred, axis=-1)
    weights = jax.nn.softmax(scores, axis=-1) * block_live[:, None, None]
    counts = jnp.sum(weights, axis=1)
    totals = jnp.einsum('bpk,bpi->bki', weights, rows_float, precision=highest)
    weighted = weights[:, :, :, None] * rows_float[:, :, None, :]
    second = jnp.einsum('bpki,bpj->bkij', weighted, rows_float, precision=highest)
    return (counts, totals, second)

def class_members(class_lists, list_counts, block_total):
    positions = jnp.arange(class_lists.shape[1], dtype=jnp.int32)
    member = (class_lists[:, :, None] == jnp.arange(block_total, dtype=jnp.int32)[None, None, :]) & (positions[None, :, None] < list_counts[:, None, None])
    present = jnp.any(member, axis=1)
    class_ids = jnp.arange(class_lists.shape[0], dtype=jnp.int32)
    block_class = jnp.sum(jnp.where(present, class_ids[:, None], 0), axis=0).astype(jnp.int32)
    onehot = present.astype(jnp.float32)
    return (onehot, block_class, jnp.sum(onehot, axis=0))

def class_reduce(onehot, counts, totals, second):
    return (jnp.einsum('cb,bk->ck', onehot, counts, precision=highest), jnp.einsum('cb,bki->cki', onehot, totals, precision=highest), jnp.einsum('cb,bkij->ckij', onehot, second, precision=highest))

def update(counts, totals, second, mean_old):
    width = totals.shape[-1]
    denom = counts + prior_weight
    new_mean = (totals + prior_weight * mean_old) / denom[:, None]
    scatter = second + prior_weight * mean_old[:, :, None] * mean_old[:, None, :] - denom[:, None, None] * new_mean[:, :, None] * new_mean[:, None, :]
    identity = jnp.eye(width, dtype=jnp.float32)
    covariance = (scatter + prior_spread * identity) / denom[:, None, None]
    lower_factor = jnp.linalg.cholesky(covariance)
    inverse = jax.scipy.linalg.solve_triangular(lower_factor, jnp.broadcast_to(identity, covariance.shape), lower=True)
    return (new_mean, jnp.swapaxes(inverse, 1, 2))

def reference(embeddings, class_blocks, class_counts, means, log_weights, factors):
    factors_float = factors.astype(jnp.float32)
    mean_proj = jnp.einsum('cki,ckij->ckj', means, factors_float, precision=highest)
    log_const = log_weights + jnp.sum(jnp.log(jnp.diagonal(factors_float, axis1=2, axis2=3)), axis=-1)
    device_total = N_TM * N_SPACE
    blocks_all = embeddings.reshape(N_TM, FR_DEV, N_SPACE, PIX_DEV // BLOCK, BLOCK, D)
    blocks_all = jnp.transpose(blocks_all, (0, 2, 1, 3, 4, 5)).reshape(device_total, NBLK, BLOCK, D)
    lists_all = class_blocks.reshape(device_total, C, CAP)
    counts_all = class_counts.reshape(device_total, C)
    start_state = (jnp.zeros((C, K), jnp.float32), jnp.zeros((C, K, D), jnp.float32), jnp.zeros((C, K, D, D), jnp.float32))

    def accumulate(carried, item):
        block_rows, class_lists, list_counts = item
        onehot, block_class, block_live = class_members(class_lists, list_counts, NBLK)
        terms = block_stats(block_rows, block_class, block_live, factors, mean_proj, log_const)
        reduced = class_reduce(onehot, *terms)
        return (tuple((old_part + new_part for old_part, new_part in zip(carried, reduced))), None)
    (counts, totals, second), _ = lax.scan(accumulate, start_state, (blocks_all, lists_all, counts_all))
    pair_count = C * K
    new_mean, new_factor = update(counts.reshape(pair_count), totals.reshape(pair_count, D), second.reshape(pair_count, D, D), means.reshape(pair_count, D))
    new_log = jnp.log(counts + 1.0) - jnp.log(jnp.sum(counts, axis=1, keepdims=True) + K)
    return (new_log, new_mean.reshape(C, K, D), new_factor.reshape(C, K, D, D))
```

```python
import functools
import jax
import jax.numpy as jnp
from jax import lax
from jax.experimental import pallas as pl
from jax.experimental.pallas import tpu as pltpu
from jax.sharding import Mesh, PartitionSpec as P

CLASSES = 19
COMPS = 5
WIDTH = 128
BLOCK = 128
ROWS = 72
STRIPS = 16
F32 = jnp.float32
BF16 = jnp.bfloat16
SLOTS = 96
HALF = 48
VMEM_LIMIT = 48 * 1024 * 1024


def iota(shape, axis):
    return lax.broadcasted_iota(jnp.int32, shape, axis)


def pieces(value, count):
    out = []
    for _ in range(count):
        part = value.astype(BF16)
        out.append(part)
        value = value - part.astype(F32)
    return out


def pack_strips(strips, extra):
    lane = iota((8, WIDTH), 1)
    out = [strips[0]]
    for s in range(1, 8):
        moved = pltpu.roll(strips[16 - s], 8 * s, 1)
        out.append(jnp.where(lane >= 8 * s, strips[s], moved))
    out.append(jnp.where(lane >= 64, strips[8], extra))
    return out


def unpack_strips(slots):
    lane = iota((8, WIDTH), 1)
    strips = [None] * 16
    strips[0] = slots[0]
    for s in range(1, 8):
        strips[s] = jnp.where(lane >= 8 * s, slots[s], 0.0)
        moved = pltpu.roll(slots[s], WIDTH - 8 * s, 1)
        strips[16 - s] = jnp.where(lane >= WIDTH - 8 * s, moved, 0.0)
    strips[8] = jnp.where(lane >= 64, slots[8], 0.0)
    return strips


def extra_rows(row, count):
    sub = iota((8, WIDTH), 0)
    later = pltpu.roll(jnp.broadcast_to(row, (8, WIDTH)), 64, 1)
    return jnp.where(sub == 0, row, jnp.where(sub == 1, later, jnp.where(sub == 2, count, 0.0)))


def split_extra(slot):
    lane = iota((8, WIDTH), 1)
    moved = pltpu.roll(slot, 64, 1)
    row = jnp.where(lane[0:1] < 64, slot[0:1], moved[1:2])
    count = jnp.where(lane[0:1] < 64, slot[2:3], moved[2:3])
    return row, count


def moments_kernel(lists, list_counts, core, lw_ref, emb_ref, fac_ref, mean_ref, own_ref, other_ref, acc, tot, cnt):
    c = pl.program_id(0)
    n = list_counts[c]
    acc[...] = jnp.zeros_like(acc)
    tot[...] = jnp.zeros_like(tot)
    cnt[...] = jnp.zeros_like(cnt)

    @pl.when(n > 0)
    def _():
        eye = iota((WIDTH, WIDTH), 0) == iota((WIDTH, WIDTH), 1)
        sub = iota((8, WIDTH), 0)
        mean = mean_ref[0]
        mean_pieces = jnp.concatenate(
            pieces(jnp.concatenate([mean, jnp.zeros((16 - COMPS, WIDTH), F32)]), 3)
        )
        diag = jnp.ones((8, WIDTH), F32)
        lw = jnp.full((8, WIDTH), -1e30, F32)
        mean_proj = []
        for k in range(COMPS):
            factor = fac_ref[0, k]
            diag_row = jnp.sum(jnp.where(eye, factor.astype(F32), 0.0), axis=0, keepdims=True)
            diag = jnp.where(sub == k, diag_row, diag)
            lw = jnp.where(sub == k, lw_ref[c, k], lw)
            parts = jnp.dot(mean_pieces, factor, preferred_element_type=F32)
            mean_proj.append(parts[k : k + 1] + parts[16 + k : 17 + k] + parts[32 + k : 33 + k])
        log_const = lw[:, 0:1] + jnp.sum(jnp.log(diag), axis=1, keepdims=True)
        selector = jnp.where(
            (iota((16, COMPS * WIDTH), 1) // WIDTH) == iota((16, COMPS * WIDTH), 0), 1.0, 0.0
        ).astype(BF16)

        def step(t, carry):
            first = emb_ref[lists[c, 2 * t]]
            later = emb_ref[lists[c, 2 * t + 1]]
            rows = jnp.concatenate([first, later], axis=0)
            rows_t = jnp.concatenate([first.astype(F32).T, later.astype(F32).T], axis=1)
            squares = []
            for k in range(COMPS):
                centred = jnp.dot(rows, fac_ref[0, k], preferred_element_type=F32) - mean_proj[k]
                squares.append(centred * centred)
            square = jnp.concatenate(squares, axis=1)
            total = None
            for part in pieces(square, 3):
                term = lax.dot_general(
                    selector, part, (((1,), (1,)), ((), ())), preferred_element_type=F32
                )
                total = term if total is None else total + term
            scores = log_const - 0.5 * total[0:8]
            top = jnp.max(scores, axis=0, keepdims=True)
            weights = jnp.exp(scores - top)
            weights = weights / jnp.sum(weights, axis=0, keepdims=True)
            live = (iota((8, 2 * BLOCK), 1) < BLOCK) | (2 * t + 1 < n)
            weights = jnp.where(live, weights, 0.0)
            both = jnp.concatenate([rows, rows], axis=0)
            for k in range(COMPS):
                scaled = rows_t * weights[k : k + 1]
                high, low = pieces(scaled, 2)
                acc[k] += jnp.dot(
                    jnp.concatenate([high, low], axis=1), both, preferred_element_type=F32
                )
            tall = jnp.concatenate([weights, jnp.zeros_like(weights)])
            sums = jnp.dot(jnp.concatenate(pieces(tall, 3)), rows, preferred_element_type=F32)
            tot[...] += sums[0:8] + sums[16:24] + sums[32:40]
            cnt[...] += weights[:, :BLOCK] + weights[:, BLOCK:]
            return carry

        lax.fori_loop(0, (n + 1) // 2, step, 0)

    count = jnp.broadcast_to(jnp.sum(cnt[...], axis=1, keepdims=True), (8, WIDTH))
    totals = tot[...]
    for k in range(COMPS):
        slots = pack_strips(
            [acc[k, 8 * s : 8 * s + 8, :] for s in range(STRIPS)],
            extra_rows(totals[k : k + 1], count[k : k + 1]),
        )
        packed = jnp.concatenate(slots, axis=0)
        slot = c * COMPS + k
        mine = (slot >= HALF) == (core[0] == 1)
        place = lax.rem(slot, HALF)

        @pl.when(mine)
        def _():
            own_ref[place] = packed

        @pl.when(jnp.logical_not(mine))
        def _():
            other_ref[place] = packed

    @pl.when(c == CLASSES - 1)
    def _():
        @pl.when(core[0] == 1)
        def _():
            own_ref[HALF - 1] = jnp.zeros((ROWS, WIDTH), F32)

        @pl.when(core[0] == 0)
        def _():
            other_ref[HALF - 1] = jnp.zeros((ROWS, WIDTH), F32)


def local_moments(blocks, lists, list_counts, core, log_weights, factors, means):
    whole = pl.BlockSpec((HALF, ROWS, WIDTH), lambda c, *_: (0, 0, 0))
    return pl.pallas_call(
        moments_kernel,
        grid_spec=pltpu.PrefetchScalarGridSpec(
            num_scalar_prefetch=3,
            grid=(CLASSES,),
            in_specs=[
                pl.BlockSpec(memory_space=pltpu.SMEM),
                pl.BlockSpec(blocks.shape, lambda c, *_: (0, 0, 0)),
                pl.BlockSpec((1, COMPS, WIDTH, WIDTH), lambda c, *_: (c, 0, 0, 0)),
                pl.BlockSpec((1, COMPS, WIDTH), lambda c, *_: (c, 0, 0)),
            ],
            out_specs=[whole, whole],
            scratch_shapes=[
                pltpu.VMEM((COMPS, WIDTH, WIDTH), F32),
                pltpu.VMEM((8, WIDTH), F32),
                pltpu.VMEM((8, WIDTH), F32),
            ],
        ),
        out_shape=[jax.ShapeDtypeStruct((HALF, ROWS, WIDTH), F32)] * 2,
        compiler_params=pltpu.CompilerParams(vmem_limit_bytes=VMEM_LIMIT),
        name="moments",
    )(lists, list_counts, core, log_weights, blocks, factors, means)


def solve_kernel(first, share_ref, mean_ref, out_ref):
    group = share_ref.shape[0]
    lane = iota((8, WIDTH), 1)
    sub = iota((8, WIDTH), 0)
    eye = iota((WIDTH, WIDTH), 0) == iota((WIDTH, WIDTH), 1)
    strips, new_means, counts = [], [], []
    for g in range(group):
        slots = [share_ref[g, 8 * s : 8 * s + 8, :] for s in range(9)]
        totals, count = split_extra(slots[8])
        old = mean_ref[pl.ds(jnp.minimum(first[0] + g, CLASSES * COMPS - 1), 1), :]
        denom = count + 1.0
        new = (totals + old) / denom
        old_t = jnp.broadcast_to(old, (WIDTH, WIDTH)).T
        new_t = jnp.broadcast_to(new * denom, (WIDTH, WIDTH)).T
        second = unpack_strips(slots)
        rows = []
        for s in range(STRIPS):
            cut = slice(8 * s, 8 * s + 8)
            scatter = second[s] + old_t[cut] * old - new_t[cut] * new
            scatter = jnp.where(lane - 8 * s == sub, scatter + 1.0, scatter)
            rows.append(jnp.where(lane >= 8 * s, scatter / denom, 0.0))
        strips.append(rows)
        new_means.append(new)
        counts.append(count)
    for s in range(STRIPS):
        for g in range(group):
            rows = strips[g]
            panel = rows[s]
            columns = [
                jnp.broadcast_to(panel[:, 8 * s + j : 8 * s + j + 1], (8, WIDTH)) for j in range(8)
            ]
            block = (lane >= 8 * s) & (lane < 8 * s + 8)
            panel = jnp.where(block, jnp.where(lane - 8 * s == sub, 1.0, 0.0), panel)
            pivots = jnp.ones((8, WIDTH), F32)
            for j in range(8):
                pivot = columns[j][j : j + 1]
                pivots = jnp.where(sub == j, pivot, pivots)
                if j < 7:
                    ratio = jnp.where(sub > j, columns[j] * (1.0 / pivot), 0.0)
                    panel = panel - ratio * panel[j : j + 1]
                    for l in range(j + 1, 8):
                        columns[l] = columns[l] - ratio * columns[l][j : j + 1]
            panel = panel * (1.0 / jnp.sqrt(pivots))
            rows[s] = panel
            if s < STRIPS - 1:
                a, b, d = [p.astype(F32) for p in pieces(panel, 3)]
                left = jnp.concatenate([a, a, b, b, a, d], axis=0).astype(BF16)
                right = jnp.concatenate([a, b, a, b, d, a], axis=0).astype(BF16)
                change = lax.dot_general(
                    left, right, (((0,), (0,)), ((), ())), preferred_element_type=F32
                )
                for t in range(s + 1, STRIPS):
                    base = jnp.where(block, 0.0, rows[t])
                    rows[t] = base - change[8 * t : 8 * t + 8]
    for g in range(group):
        lower = jnp.concatenate(
            [jnp.where(lane - 8 * s <= sub, strips[g][s], 0.0) for s in range(STRIPS)], axis=0
        )
        upper = lower.T
        slots = pack_strips(
            [upper[8 * s : 8 * s + 8] for s in range(STRIPS)],
            extra_rows(new_means[g], counts[g]),
        )
        out_ref[g] = jnp.concatenate(slots, axis=0)


def solve_share(first, share, means):
    return pl.pallas_call(
        solve_kernel,
        in_specs=[
            pl.BlockSpec(memory_space=pltpu.SMEM),
            pl.BlockSpec(memory_space=pltpu.VMEM),
            pl.BlockSpec(memory_space=pltpu.VMEM),
        ],
        out_specs=pl.BlockSpec(memory_space=pltpu.VMEM),
        out_shape=jax.ShapeDtypeStruct(share.shape, F32),
        compiler_params=pltpu.CompilerParams(vmem_limit_bytes=VMEM_LIMIT),
        name="solve",
    )(first, share, means)


def unpack_kernel(packed_ref, factor_ref, mean_ref, count_ref):
    group = packed_ref.shape[0]
    for g in range(group):
        slots = [packed_ref[g, 8 * s : 8 * s + 8, :] for s in range(9)]
        strips = unpack_strips(slots)
        for s in range(STRIPS):
            factor_ref[g, 8 * s : 8 * s + 8, :] = strips[s]
        row, count = split_extra(slots[8])
        mean_ref[0, g : g + 1, :] = row
        count_ref[0, g : g + 1, :] = count


def unpack_all(packed):
    group = 19
    steps = CLASSES * COMPS // group
    return pl.pallas_call(
        unpack_kernel,
        grid=(steps,),
        in_specs=[pl.BlockSpec((group, ROWS, WIDTH), lambda i: (i, 0, 0))],
        out_specs=[
            pl.BlockSpec((group, WIDTH, WIDTH), lambda i: (i, 0, 0)),
            pl.BlockSpec((1, group, WIDTH), lambda i: (i, 0, 0)),
            pl.BlockSpec((1, group, WIDTH), lambda i: (i, 0, 0)),
        ],
        out_shape=[
            jax.ShapeDtypeStruct((CLASSES * COMPS, WIDTH, WIDTH), F32),
            jax.ShapeDtypeStruct((steps, group, WIDTH), F32),
            jax.ShapeDtypeStruct((steps, group, WIDTH), F32),
        ],
        compiler_params=pltpu.CompilerParams(vmem_limit_bytes=VMEM_LIMIT),
        name="unpack",
    )(packed)


def spread(value, axes, count):
    return lax.all_to_all(
        jnp.broadcast_to(value[None], (count,) + value.shape), axes, 0, 0, tiled=True
    )


def body(embeddings, class_blocks, class_counts, means, log_weights, factors):
    frames_here, pixels_here, width = embeddings.shape
    blocks = embeddings.reshape(frames_here * pixels_here // BLOCK, BLOCK, width)
    core = lax.axis_index("core").astype(jnp.int32)
    own, other = local_moments(
        blocks, class_blocks[0, 0], class_counts[0, 0], core[None], log_weights, factors, means
    )
    half = own + lax.ppermute(other, "core", [(0, 1), (1, 0)])
    group = HALF // 16
    parts = lax.all_to_all(half, ("x", "y"), 0, 0, tiled=True)
    share = jnp.sum(parts.reshape(16, group, ROWS, WIDTH), axis=0)
    rows = group * ROWS // 8
    parts = lax.all_to_all(share.reshape(8, rows, WIDTH), "z", 0, 0, tiled=True)
    share = spread(jnp.sum(parts, axis=0), "z", 8).reshape(group, ROWS, WIDTH)
    place = lax.axis_index("x") * 4 + lax.axis_index("y")
    first = (core * HALF + place * group).astype(jnp.int32)
    solved = solve_share(first[None], share, means.reshape(CLASSES * COMPS, width))
    here = spread(solved, ("x", "y"), 16).reshape(HALF, ROWS, WIDTH)
    there = lax.ppermute(here, "core", [(0, 1), (1, 0)])
    packed = jnp.where(
        core == 0, jnp.concatenate([here, there]), jnp.concatenate([there, here])
    )
    new_factor, new_mean, counts = unpack_all(packed)
    counts = counts.reshape(CLASSES, COMPS, width)[:, :, 0]
    new_log = jnp.log(counts + 1.0) - jnp.log(jnp.sum(counts, axis=1, keepdims=True) + COMPS)
    return (
        new_log,
        new_mean.reshape(CLASSES, COMPS, width),
        new_factor.reshape(CLASSES, COMPS, width, width),
    )


def solution(mesh):
    wide = Mesh(mesh.devices.reshape(4, 8, 4, 2), ("x", "z", "y", "core"))
    space = ("z", "y", "core")
    return jax.shard_map(
        body,
        mesh=wide,
        in_specs=(P("x", space, None), P("x", space, None, None), P("x", space, None), P(), P(), P()),
        out_specs=(P(), P(), P()),
        check_vma=False,
    )
```

```python
import functools
import jax
import jax.numpy as jnp
from jax import lax
from jax.experimental import pallas as pl
from jax.experimental.pallas import tpu as pltpu
from jax.sharding import Mesh, PartitionSpec as P

CLASSES = 19
COMPS = 5
WIDTH = 128
BLOCK = 128
ROWS = 72
STRIPS = 16
F32 = jnp.float32
BF16 = jnp.bfloat16
SLOTS = 9
GROUP = 3
OWNERS = 16
HALF = GROUP * OWNERS
SHARE = 224
PART = SHARE // 2
VMEM_LIMIT = 48 * 1024 * 1024


def iota(shape, axis):
    return lax.broadcasted_iota(jnp.int32, shape, axis)


def pieces(value, count):
    out = []
    for _ in range(count):
        part = value.astype(BF16)
        out.append(part)
        value = value - part.astype(F32)
    return out


def pack_strips(strips, extra):
    lane = iota((8, WIDTH), 1)
    out = [strips[0]]
    for s in range(1, 8):
        moved = pltpu.roll(strips[16 - s], 8 * s, 1)
        out.append(jnp.where(lane >= 8 * s, strips[s], moved))
    out.append(jnp.where(lane >= 64, strips[8], extra))
    return out


def unpack_strips(slots):
    lane = iota((8, WIDTH), 1)
    strips = [None] * 16
    strips[0] = slots[0]
    for s in range(1, 8):
        strips[s] = jnp.where(lane >= 8 * s, slots[s], 0.0)
        moved = pltpu.roll(slots[s], WIDTH - 8 * s, 1)
        strips[16 - s] = jnp.where(lane >= WIDTH - 8 * s, moved, 0.0)
    strips[8] = jnp.where(lane >= 64, slots[8], 0.0)
    return strips


def extra_rows(row, count):
    sub = iota((8, WIDTH), 0)
    later = pltpu.roll(jnp.broadcast_to(row, (8, WIDTH)), 64, 1)
    return jnp.where(sub == 0, row, jnp.where(sub == 1, later, jnp.where(sub == 2, count, 0.0)))


def split_extra(slot):
    lane = iota((8, WIDTH), 1)
    moved = pltpu.roll(slot, 64, 1)
    row = jnp.where(lane[0:1] < 64, slot[0:1], moved[1:2])
    count = jnp.where(lane[0:1] < 64, slot[2:3], moved[2:3])
    return row, count


def moments_kernel(lists, list_counts, core, lw_ref, emb_ref, fac_ref, mean_ref, own_ref, other_ref,
                   acc, tot, cnt, flipped, shift, const, rows_t, gate, items):
    sub = iota((8, WIDTH), 0)
    lane = iota((8, WIDTH), 1)
    ident = (iota((WIDTH, WIDTH), 0) == iota((WIDTH, WIDTH), 1)).astype(F32).astype(BF16)

    acc[...] = jnp.zeros_like(acc)
    tot[...] = jnp.zeros_like(tot)
    cnt[...] = jnp.zeros_like(cnt)
    gate[...] = jnp.zeros_like(gate)
    rows_t[...] = jnp.zeros_like(rows_t)

    def list_class(c, at):
        n = list_counts[c]

        def list_pair(t, at):
            items[0, at] = c
            items[1, at] = lists[2 * t, c]
            items[2, at] = lists[2 * t + 1, c]
            items[3, at] = jnp.where(2 * t + 1 < n, 2 * BLOCK, BLOCK)
            return at + 1

        return lax.fori_loop(0, (n + 1) // 2, list_pair, at)

    total_items = lax.fori_loop(0, CLASSES, list_class, jnp.int32(0))

    def half_step(i, now, before):
        at_sum = jnp.minimum(jnp.maximum(i - 2, 0), total_items - 1)
        at_score = jnp.minimum(jnp.maximum(i - 1, 0), total_items - 1)
        at_class = jnp.minimum(i, total_items - 1)

        c = items[0, at_sum]
        rows = jnp.concatenate([emb_ref[items[1, at_sum]], emb_ref[items[2, at_sum]]], axis=0)
        weights = gate[before]
        flat = rows_t[before]
        both = jnp.concatenate([rows, rows], axis=0)
        scaled = []
        for k in range(COMPS):
            high, low = pieces(flat * weights[k : k + 1], 2)
            scaled.append(jnp.concatenate([high, low], axis=1))
        for k in range(COMPS):
            acc[c * COMPS + k] += jnp.dot(scaled[k], both, preferred_element_type=F32)
        tall = jnp.concatenate([weights, jnp.zeros_like(weights)])
        sums = jnp.dot(jnp.concatenate(pieces(tall, 3)), rows, preferred_element_type=F32)
        tot[c] += sums[0:8] + sums[16:24] + sums[32:40]
        cnt[c] += weights[:, :BLOCK] + weights[:, BLOCK:]

        first = emb_ref[items[1, at_score]].astype(F32).T
        later = emb_ref[items[2, at_score]].astype(F32).T
        flat = jnp.concatenate([first, later], axis=1)
        square = jnp.zeros((8, 2 * BLOCK), F32)
        wide_sub = iota((8, 2 * BLOCK), 0)
        flat_half = flat.astype(BF16)
        for k in range(COMPS):
            offset = shift[before, k]
            centred = jnp.dot(flipped[before, k], flat_half, preferred_element_type=F32)
            centred = centred - jnp.concatenate([offset, offset], axis=1)
            line = jnp.sum(centred * centred, axis=0, keepdims=True)
            square = jnp.where(wide_sub == k, line, square)
        consts = const[before]
        scores = jnp.concatenate([consts, consts], axis=1) - 0.5 * square
        top = jnp.max(scores, axis=0, keepdims=True)
        weights = jnp.exp(scores - top)
        weights = weights / jnp.sum(weights, axis=0, keepdims=True)
        live = jnp.where((i >= 1) & (i <= total_items), items[3, at_score], 0)
        gate[now] = jnp.where(iota((8, 2 * BLOCK), 1) < live, weights, 0.0)
        rows_t[now] = flat

        c = items[0, at_class]
        diag = jnp.ones((8, WIDTH), F32)
        prior = jnp.full((8, WIDTH), -1e30, F32)
        mean = mean_ref[:, c]
        mean_pieces = jnp.concatenate(
            pieces(jnp.concatenate([mean, jnp.zeros((16 - COMPS, WIDTH), F32)]), 3)
        )
        for k in range(COMPS):
            factor = fac_ref[c, k]
            wide = factor.astype(F32)
            on_diag = None
            for s in range(STRIPS):
                part = jnp.where(lane - 8 * s == sub, wide[8 * s : 8 * s + 8], 0.0)
                on_diag = part if on_diag is None else on_diag + part
            diag = jnp.where(sub == k, jnp.sum(on_diag, axis=0, keepdims=True), diag)
            prior = jnp.where(sub == k, lw_ref[k, c], prior)
            flipped[now, k] = wide.T.astype(BF16)
            parts = jnp.dot(mean_pieces, factor, preferred_element_type=F32)
            line = parts[k : k + 1] + parts[16 + k : 17 + k] + parts[32 + k : 33 + k]
            shift[now, k] = jnp.broadcast_to(line, (WIDTH, WIDTH)).T
        const[now] = jnp.sum(jnp.log(diag), axis=1, keepdims=True) + prior

    def step(i, carry):
        half_step(2 * i, 0, 1)
        half_step(2 * i + 1, 1, 0)
        return carry

    lax.fori_loop(0, (total_items + 3) // 2, step, 0)

    def pack(q, carry):
        for base, out_ref in ((core[0], own_ref), (1 - core[0], other_ref)):
            for r in range(GROUP):
                slot = base * HALF + q * GROUP + r
                c = slot // COMPS
                k = slot - c * COMPS
                counted = cnt[c, pl.ds(k, 1), :]
                count = jnp.broadcast_to(jnp.sum(counted, axis=1, keepdims=True), (1, WIDTH))
                slots = pack_strips(
                    [acc[slot, 8 * s : 8 * s + 8, :] for s in range(STRIPS)],
                    extra_rows(tot[c, pl.ds(k, 1), :], count),
                )
                for s in range(SLOTS):
                    out_ref[q, r * ROWS + 8 * s : r * ROWS + 8 * s + 8, :] = slots[s]
            out_ref[q, GROUP * ROWS : SHARE, :] = jnp.zeros((SHARE - GROUP * ROWS, WIDTH), F32)
        return carry

    lax.fori_loop(0, OWNERS, pack, 0)


def local_moments(blocks, lists, list_counts, core, log_weights, factors, means):
    vmem = pl.BlockSpec(memory_space=pltpu.VMEM)
    smem = pl.BlockSpec(memory_space=pltpu.SMEM)
    return pl.pallas_call(
        moments_kernel,
        in_specs=[smem, smem, smem, smem, vmem, vmem, vmem],
        out_specs=[vmem, vmem],
        scratch_shapes=[
            pltpu.VMEM(((CLASSES + 1) * COMPS, WIDTH, WIDTH), F32),
            pltpu.VMEM((CLASSES + 1, 8, WIDTH), F32),
            pltpu.VMEM((CLASSES + 1, 8, WIDTH), F32),
            pltpu.VMEM((2, COMPS, WIDTH, WIDTH), BF16),
            pltpu.VMEM((2, COMPS, WIDTH, WIDTH), F32),
            pltpu.VMEM((2, 8, WIDTH), F32),
            pltpu.VMEM((2, WIDTH, 2 * BLOCK), F32),
            pltpu.VMEM((2, 8, 2 * BLOCK), F32),
            pltpu.SMEM((4, 128), jnp.int32),
        ],
        out_shape=[jax.ShapeDtypeStruct((OWNERS, SHARE, WIDTH), F32)] * 2,
        compiler_params=pltpu.CompilerParams(vmem_limit_bytes=VMEM_LIMIT),
        name="moments",
    )(lists, list_counts, core, log_weights, blocks, factors, means)


def solve_kernel(place, mine_ref, theirs_ref, mean_ref, out_ref):
    lane = iota((8, WIDTH), 1)
    sub = iota((8, WIDTH), 0)
    early = place[1] == 0
    share = []
    for at in range(2):
        for t in range(PART // 8):
            cut = slice(8 * t, 8 * t + 8)
            share.append(jnp.where(early == (at == 0), mine_ref[cut, :], theirs_ref[cut, :]))
    strips, new_means, counts = [], [], []
    for g in range(GROUP):
        slots = share[SLOTS * g : SLOTS * g + SLOTS]
        totals, count = split_extra(slots[8])
        comp = jnp.minimum(place[0] + g, CLASSES * COMPS - 1)
        old = mean_ref[lax.rem(comp, COMPS), pl.ds(comp // COMPS, 1), :]
        denom = count + 1.0
        new = (totals + old) / denom
        old_t = jnp.broadcast_to(old, (WIDTH, WIDTH)).T
        new_t = jnp.broadcast_to(new * denom, (WIDTH, WIDTH)).T
        second = unpack_strips(slots)
        rows = []
        for s in range(STRIPS):
            cut = slice(8 * s, 8 * s + 8)
            scatter = second[s] + old_t[cut] * old - new_t[cut] * new
            scatter = jnp.where(lane - 8 * s == sub, scatter + 1.0, scatter)
            rows.append(jnp.where(lane >= 8 * s, scatter / denom, 0.0))
        strips.append(rows)
        new_means.append(new)
        counts.append(count)
    for s in range(STRIPS):
        for g in range(GROUP):
            rows = strips[g]
            panel = rows[s]
            columns = [
                jnp.broadcast_to(panel[:, 8 * s + j : 8 * s + j + 1], (8, WIDTH)) for j in range(8)
            ]
            block = (lane >= 8 * s) & (lane < 8 * s + 8)
            panel = jnp.where(block, jnp.where(lane - 8 * s == sub, 1.0, 0.0), panel)
            pivots = jnp.ones((8, WIDTH), F32)
            for j in range(8):
                pivot = columns[j][j : j + 1]
                pivots = jnp.where(sub == j, pivot, pivots)
                if j < 7:
                    ratio = jnp.where(sub > j, columns[j] * (1.0 / pivot), 0.0)
                    panel = panel - ratio * panel[j : j + 1]
                    for l in range(j + 1, 8):
                        columns[l] = columns[l] - ratio * columns[l][j : j + 1]
            panel = panel * (1.0 / jnp.sqrt(pivots))
            rows[s] = panel
            if s < STRIPS - 1:
                a, b, d = [p.astype(F32) for p in pieces(panel, 3)]
                left = jnp.concatenate([a, a, b, b, a, d], axis=0).astype(BF16)
                right = jnp.concatenate([a, b, a, b, d, a], axis=0).astype(BF16)
                change = lax.dot_general(
                    left, right, (((0,), (0,)), ((), ())), preferred_element_type=F32
                )
                for t in range(s + 1, STRIPS):
                    base = jnp.where(block, 0.0, rows[t])
                    rows[t] = base - change[8 * t : 8 * t + 8]
    packed = []
    for g in range(GROUP):
        lower = jnp.concatenate(
            [jnp.where(lane - 8 * s <= sub, strips[g][s], 0.0) for s in range(STRIPS)], axis=0
        )
        upper = lower.T
        packed += pack_strips(
            [upper[8 * s : 8 * s + 8] for s in range(STRIPS)],
            extra_rows(new_means[g], counts[g]),
        )
    packed.append(jnp.zeros((8, WIDTH), F32))
    for t in range(PART // 8):
        out_ref[8 * t : 8 * t + 8, :] = jnp.where(early, packed[t], packed[PART // 8 + t])


def solve_share(place, mine, theirs, means):
    smem = pl.BlockSpec(memory_space=pltpu.SMEM)
    vmem = pl.BlockSpec(memory_space=pltpu.VMEM)
    return pl.pallas_call(
        solve_kernel,
        in_specs=[smem, vmem, vmem, vmem],
        out_specs=vmem,
        out_shape=jax.ShapeDtypeStruct((PART, WIDTH), F32),
        compiler_params=pltpu.CompilerParams(vmem_limit_bytes=VMEM_LIMIT),
        name="solve",
    )(place, mine, theirs, means)


UNPACK = 19


def unpack_kernel(core, here_ref, there_ref, factor_ref, mean_ref, log_ref, counts):
    step = pl.program_id(0)
    for g in range(UNPACK):
        comp = step * UNPACK + g
        half = jnp.where(comp >= HALF, 1, 0)
        at = comp - half * HALF
        q = at // GROUP
        first = pl.multiple_of((at - q * GROUP) * ROWS, 8)
        here = half == core[0]
        slots = []
        for s in range(SLOTS):
            cut = pl.ds(first + 8 * s, 8)
            slots.append(jnp.where(here, here_ref[q, cut, :], there_ref[q, cut, :]))
        strips = unpack_strips(slots)
        for s in range(STRIPS):
            factor_ref[g, 8 * s : 8 * s + 8, :] = strips[s]
        row, count = split_extra(slots[8])
        c = comp // COMPS
        k = comp - c * COMPS
        mean_ref[k, pl.ds(c, 1), :] = row
        counts[k, pl.ds(c, 1), :] = count

    @pl.when(step == CLASSES * COMPS // UNPACK - 1)
    def _():
        mask = iota((CLASSES, WIDTH), 0) == iota((CLASSES, WIDTH), 1)
        values = [counts[k] for k in range(COMPS)]
        total = jnp.log(sum(values) + float(COMPS))
        for k in range(COMPS):
            logs = jnp.where(mask, jnp.log(values[k] + 1.0) - total, 0.0)
            log_ref[k : k + 1, :] = jnp.sum(logs, axis=0, keepdims=True)[:, :CLASSES]


def unpack_all(core, here, there):
    steps = CLASSES * COMPS // UNPACK
    vmem = pl.BlockSpec(memory_space=pltpu.VMEM)
    return pl.pallas_call(
        unpack_kernel,
        grid=(steps,),
        in_specs=[pl.BlockSpec(memory_space=pltpu.SMEM), vmem, vmem],
        out_specs=[
            pl.BlockSpec((UNPACK, WIDTH, WIDTH), lambda i: (i, 0, 0)),
            pl.BlockSpec((COMPS, CLASSES, WIDTH), lambda i: (0, 0, 0)),
            pl.BlockSpec((COMPS, CLASSES), lambda i: (0, 0)),
        ],
        out_shape=[
            jax.ShapeDtypeStruct((CLASSES * COMPS, WIDTH, WIDTH), F32),
            jax.ShapeDtypeStruct((COMPS, CLASSES, WIDTH), F32),
            jax.ShapeDtypeStruct((COMPS, CLASSES), F32),
        ],
        scratch_shapes=[pltpu.VMEM((COMPS, CLASSES, WIDTH), F32)],
        compiler_params=pltpu.CompilerParams(vmem_limit_bytes=VMEM_LIMIT),
        name="unpack",
    )(core, here, there)


def swap_cores(value):
    return lax.ppermute(value, "core", [(0, 1), (1, 0)])


def sum_far(value):
    total = value
    for hop in (2, 1, 3):
        total = total + lax.ppermute(value, "far", [(i, (i + hop) % 4) for i in range(4)])
    return total


def body(embeddings, class_blocks, class_counts, means, log_weights, factors):
    frames_here, pixels_here, width = embeddings.shape
    blocks = embeddings.reshape(frames_here * pixels_here // BLOCK, BLOCK, width)
    core = lax.axis_index("core").astype(jnp.int32)
    near = lax.axis_index("near").astype(jnp.int32)
    owner = (lax.axis_index("x") * 4 + lax.axis_index("y")).astype(jnp.int32)
    means_t = jnp.transpose(means, (1, 0, 2))
    own, other = local_moments(
        blocks, class_blocks[0, 0].T, class_counts[0, 0], core[None], log_weights.T, factors, means_t
    )
    peers = ("x", "y", "near")
    half = own + swap_cores(other)
    parts = lax.all_to_all(half.reshape(2 * OWNERS, PART, width), peers, 0, 0, tiled=True)
    mine = sum_far(jnp.sum(parts, axis=0))
    theirs = lax.ppermute(mine, "near", [(0, 1), (1, 0)])
    place = jnp.stack([core * HALF + owner * GROUP, near])
    solved = solve_share(place, mine, theirs, means_t)
    spread = jnp.broadcast_to(solved[None], (2 * OWNERS, PART, width))
    here = lax.all_to_all(spread, peers, 0, 0, tiled=True).reshape(OWNERS, SHARE, width)
    there = swap_cores(here)
    new_factor, new_mean, new_log = unpack_all(core[None], here, there)
    return (
        new_log.T,
        jnp.transpose(new_mean, (1, 0, 2)),
        new_factor.reshape(CLASSES, COMPS, width, width),
    )


def solution(mesh):
    wide = Mesh(mesh.devices.reshape(4, 4, 2, 4, 2), ("x", "far", "near", "y", "core"))
    space = ("far", "near", "y", "core")
    return jax.shard_map(
        body,
        mesh=wide,
        in_specs=(P("x", space, None), P("x", space, None, None), P("x", space, None), P(), P(), P()),
        out_specs=(P(), P(), P()),
        check_vma=False,
    )
```

```python
import functools
import jax
import jax.numpy as jnp
from jax import lax
from jax.experimental import pallas as pl
from jax.experimental.pallas import tpu as pltpu
from jax.sharding import Mesh, PartitionSpec as P

CLASSES = 19
COMPS = 5
WIDTH = 128
BLOCK = 128
ROWS = 72
STRIPS = 16
F32 = jnp.float32
BF16 = jnp.bfloat16
SLOTS = 9
GROUP = 3
UNROLL = 2
OWNERS = 16
HALF = GROUP * OWNERS
SHARE = 224
PART = SHARE // 2
VMEM_LIMIT = 48 * 1024 * 1024


def iota(shape, axis):
    return lax.broadcasted_iota(jnp.int32, shape, axis)


def pieces(value, count):
    out = []
    for _ in range(count):
        part = value.astype(BF16)
        out.append(part)
        value = value - part.astype(F32)
    return out


def pack_strips(strips, extra):
    lane = iota((8, WIDTH), 1)
    out = [strips[0]]
    for s in range(1, 8):
        moved = pltpu.roll(strips[16 - s], 8 * s, 1)
        out.append(jnp.where(lane >= 8 * s, strips[s], moved))
    out.append(jnp.where(lane >= 64, strips[8], extra))
    return out


def unpack_strips(slots):
    lane = iota((8, WIDTH), 1)
    strips = [None] * 16
    strips[0] = slots[0]
    for s in range(1, 8):
        strips[s] = jnp.where(lane >= 8 * s, slots[s], 0.0)
        moved = pltpu.roll(slots[s], WIDTH - 8 * s, 1)
        strips[16 - s] = jnp.where(lane >= WIDTH - 8 * s, moved, 0.0)
    strips[8] = jnp.where(lane >= 64, slots[8], 0.0)
    return strips


def extra_rows(row, count):
    sub = iota((8, WIDTH), 0)
    later = pltpu.roll(jnp.broadcast_to(row, (8, WIDTH)), 64, 1)
    return jnp.where(sub == 0, row, jnp.where(sub == 1, later, jnp.where(sub == 2, count, 0.0)))


def split_extra(slot):
    lane = iota((8, WIDTH), 1)
    moved = pltpu.roll(slot, 64, 1)
    row = jnp.where(lane[0:1] < 64, slot[0:1], moved[1:2])
    count = jnp.where(lane[0:1] < 64, slot[2:3], moved[2:3])
    return row, count


def moments_kernel(place, lists_any, counts_any, lw_any, emb_any, fac_any, mean_any, own_any, other_any,
                   acc, tot, cnt, flipped, shift, const, rows_t, gate, items,
                   lists, list_counts, lw_ref, emb_ref, fac_ref, mean_ref, own_ref, other_ref, sems,
                   out_sems):
    pairs = ((lists_any, lists), (counts_any, list_counts), (lw_any, lw_ref), (emb_any, emb_ref),
             (fac_any, fac_ref), (mean_any, mean_ref))
    copies = [pltpu.make_async_copy(src, dst, sems.at[n]) for n, (src, dst) in enumerate(pairs)]
    for copy in copies:
        copy.start()
    sub = iota((8, WIDTH), 0)
    lane = iota((8, WIDTH), 1)
    ident = (iota((WIDTH, WIDTH), 0) == iota((WIDTH, WIDTH), 1)).astype(F32).astype(BF16)

    acc[...] = jnp.zeros_like(acc)
    tot[...] = jnp.zeros_like(tot)
    cnt[...] = jnp.zeros_like(cnt)
    gate[...] = jnp.zeros_like(gate)
    rows_t[...] = jnp.zeros_like(rows_t)

    copies[0].wait()
    copies[1].wait()

    def list_class(c, at):
        n = list_counts[c]

        def list_pair(t, at):
            items[0, at] = c
            items[1, at] = lists[2 * t, c]
            items[2, at] = lists[2 * t + 1, c]
            items[3, at] = jnp.where(2 * t + 1 < n, 2 * BLOCK, BLOCK)
            return at + 1

        return lax.fori_loop(0, (n + 1) // 2, list_pair, at)

    total_items = lax.fori_loop(0, CLASSES, list_class, jnp.int32(0))

    for copy in copies[2:]:
        copy.wait()

    def clamp(i):
        return jnp.minimum(jnp.maximum(i, 0), total_items - 1)

    def moments_of(i, u):
        at = clamp(i)
        c = items[0, at]
        rows = jnp.concatenate([emb_ref[items[1, at]], emb_ref[items[2, at]]], axis=0)
        weights = gate[u]
        flat = rows_t[u]
        both = jnp.concatenate([rows, rows], axis=0)
        for k in range(COMPS):
            high, low = pieces(flat * weights[k : k + 1], 2)
            acc[c * COMPS + k] += jnp.dot(
                jnp.concatenate([high, low], axis=1), both, preferred_element_type=F32
            )
        tall = jnp.concatenate([weights, jnp.zeros_like(weights)])
        sums = jnp.dot(jnp.concatenate(pieces(tall, 3)), rows, preferred_element_type=F32)
        tot[c] += sums[0:8] + sums[16:24] + sums[32:40]
        cnt[c] += weights[:, :BLOCK] + weights[:, BLOCK:]

    def scores_of(i, u):
        at = clamp(i)
        first = emb_ref[items[1, at]].astype(F32).T
        later = emb_ref[items[2, at]].astype(F32).T
        flat = jnp.concatenate([first, later], axis=1)
        square = jnp.zeros((8, 2 * BLOCK), F32)
        wide_sub = iota((8, 2 * BLOCK), 0)
        flat_half = flat.astype(BF16)
        offsets = shift[u].astype(BF16)
        row = iota((WIDTH, 2 * BLOCK), 0)
        for k in range(COMPS):
            ones = jnp.where((row >= 3 * k) & (row < 3 * k + 3), 1.0, 0.0).astype(BF16)
            centred = jnp.dot(
                jnp.concatenate([flipped[u, k], offsets], axis=1),
                jnp.concatenate([flat_half, ones], axis=0),
                preferred_element_type=F32,
            )
            line = jnp.sum(centred * centred, axis=0, keepdims=True)
            square = jnp.where(wide_sub == k, line, square)
        consts = const[u]
        scores = jnp.concatenate([consts, consts], axis=1) - 0.5 * square
        top = jnp.max(scores, axis=0, keepdims=True)
        weights = jnp.exp(scores - top)
        weights = weights / jnp.sum(weights, axis=0, keepdims=True)
        live = jnp.where((i >= 0) & (i < total_items), items[3, at], 0)
        gate[u] = jnp.where(iota((8, 2 * BLOCK), 1) < live, weights, 0.0)
        rows_t[u] = flat

    def prepare(i, u):
        c = items[0, clamp(i)]
        diag = jnp.ones((8, WIDTH), F32)
        prior = jnp.full((8, WIDTH), -1e30, F32)
        mean = mean_ref[:, c]
        mean_pieces = jnp.concatenate(
            pieces(jnp.concatenate([mean, jnp.zeros((16 - COMPS, WIDTH), F32)]), 3)
        )
        lines = []
        for k in range(COMPS):
            factor = fac_ref[c, k]
            wide = factor.astype(F32)
            on_diag = None
            for s in range(STRIPS):
                part = jnp.where(lane - 8 * s == sub, wide[8 * s : 8 * s + 8], 0.0)
                on_diag = part if on_diag is None else on_diag + part
            diag = jnp.where(sub == k, jnp.sum(on_diag, axis=0, keepdims=True), diag)
            prior = jnp.where(sub == k, lw_ref[k, c], prior)
            flipped[u, k] = wide.T.astype(BF16)
            parts = jnp.dot(mean_pieces, factor, preferred_element_type=F32)
            line = parts[k : k + 1] + parts[16 + k : 17 + k] + parts[32 + k : 33 + k]
            lines += [-p.astype(F32) for p in pieces(line, 3)]
        shift[u] = jnp.concatenate(lines + [jnp.zeros((WIDTH - 3 * COMPS, WIDTH), F32)], axis=0).T
        const[u] = jnp.sum(jnp.log(diag), axis=1, keepdims=True) + prior

    def step(j, carry):
        for u in range(UNROLL):
            moments_of(UNROLL * (j - 2) + u, u)
        for u in range(UNROLL):
            scores_of(UNROLL * (j - 1) + u, u)
        for u in range(UNROLL):
            prepare(UNROLL * j + u, u)
        return carry

    lax.fori_loop(0, (total_items + UNROLL - 1) // UNROLL + 2, step, 0)

    def pack(q, carry):
        for base, out_ref in ((place[0], own_ref), (1 - place[0], other_ref)):
            for r in range(GROUP):
                slot = base * HALF + q * GROUP + r
                c = slot // COMPS
                k = slot - c * COMPS
                counted = cnt[c, pl.ds(k, 1), :]
                count = jnp.broadcast_to(jnp.sum(counted, axis=1, keepdims=True), (1, WIDTH))
                slots = pack_strips(
                    [acc[slot, 8 * s : 8 * s + 8, :] for s in range(STRIPS)],
                    extra_rows(tot[c, pl.ds(k, 1), :], count),
                )
                for s in range(SLOTS):
                    out_ref[q, r * ROWS + 8 * s : r * ROWS + 8 * s + 8, :] = slots[s]
            out_ref[q, GROUP * ROWS : SHARE, :] = jnp.zeros((SHARE - GROUP * ROWS, WIDTH), F32)
        for copy in out_copies(q):
            copy.start()
        return carry

    def out_copies(q):
        return (
            pltpu.make_async_copy(own_ref.at[q], own_any.at[q], out_sems.at[0, q]),
            pltpu.make_async_copy(other_ref.at[q], other_any.at[q], out_sems.at[1, q]),
        )

    def finish(q, carry):
        for copy in out_copies(q):
            copy.wait()
        return carry

    lax.fori_loop(0, OWNERS, pack, 0)
    lax.fori_loop(0, OWNERS, finish, 0)


def local_moments(place, blocks, lists, list_counts, log_weights, factors, means):
    vmem = pl.BlockSpec(memory_space=pltpu.VMEM)
    smem = pl.BlockSpec(memory_space=pltpu.SMEM)
    anywhere = pl.BlockSpec(memory_space=pltpu.HBM)
    return pl.pallas_call(
        moments_kernel,
        in_specs=[smem] + [anywhere] * 6,
        out_specs=[anywhere, anywhere],
        scratch_shapes=[
            pltpu.VMEM(((CLASSES + 1) * COMPS, WIDTH, WIDTH), F32),
            pltpu.VMEM((CLASSES + 1, 8, WIDTH), F32),
            pltpu.VMEM((CLASSES + 1, 8, WIDTH), F32),
            pltpu.VMEM((UNROLL, COMPS, WIDTH, WIDTH), BF16),
            pltpu.VMEM((UNROLL, WIDTH, WIDTH), F32),
            pltpu.VMEM((UNROLL, 8, WIDTH), F32),
            pltpu.VMEM((UNROLL, WIDTH, 2 * BLOCK), F32),
            pltpu.VMEM((UNROLL, 8, 2 * BLOCK), F32),
            pltpu.SMEM((4, 128), jnp.int32),
            pltpu.SMEM(lists.shape, jnp.int32),
            pltpu.SMEM(list_counts.shape, jnp.int32),
            pltpu.SMEM(log_weights.shape, F32),
            pltpu.VMEM(blocks.shape, BF16),
            pltpu.VMEM(factors.shape, BF16),
            pltpu.VMEM(means.shape, F32),
            pltpu.VMEM((OWNERS, SHARE, WIDTH), F32),
            pltpu.VMEM((OWNERS, SHARE, WIDTH), F32),
            pltpu.SemaphoreType.DMA((6,)),
            pltpu.SemaphoreType.DMA((2, OWNERS)),
        ],
        out_shape=[jax.ShapeDtypeStruct((OWNERS, SHARE, WIDTH), F32)] * 2,
        compiler_params=pltpu.CompilerParams(vmem_limit_bytes=58 * 1024 * 1024),
        name="moments",
    )(place, lists, list_counts, log_weights, blocks, factors, means)


def solve_kernel(place, mine_ref, theirs_ref, mean_ref, out_ref):
    lane = iota((8, WIDTH), 1)
    sub = iota((8, WIDTH), 0)
    early = place[1] == 0
    share = []
    for at in range(2):
        for t in range(PART // 8):
            cut = slice(8 * t, 8 * t + 8)
            share.append(jnp.where(early == (at == 0), mine_ref[cut, :], theirs_ref[cut, :]))
    strips, new_means, counts = [], [], []
    for g in range(GROUP):
        slots = share[SLOTS * g : SLOTS * g + SLOTS]
        totals, count = split_extra(slots[8])
        comp = jnp.minimum(place[0] + g, CLASSES * COMPS - 1)
        old = mean_ref[lax.rem(comp, COMPS), pl.ds(comp // COMPS, 1), :]
        denom = count + 1.0
        new = (totals + old) / denom
        old_t = jnp.broadcast_to(old, (WIDTH, WIDTH)).T
        new_t = jnp.broadcast_to(new * denom, (WIDTH, WIDTH)).T
        second = unpack_strips(slots)
        full = jnp.concatenate(second, axis=0)
        mirror = full.T
        rows = []
        for s in range(STRIPS):
            cut = slice(8 * s, 8 * s + 8)
            scatter = jnp.where(lane >= 8 * s, second[s], mirror[cut])
            scatter = scatter + old_t[cut] * old - new_t[cut] * new
            scatter = jnp.where(lane - 8 * s == sub, scatter + 1.0, scatter)
            rows.append(scatter / denom)
        strips.append(rows)
        new_means.append(new)
        counts.append(count)
    for s in range(STRIPS):
        for g in range(GROUP):
            rows = strips[g]
            block = (lane >= 8 * s) & (lane < 8 * s + 8)
            panel = rows[s]
            columns = [
                jnp.broadcast_to(panel[:, 8 * s + j : 8 * s + j + 1], (8, WIDTH)) for j in range(8)
            ]
            panel = jnp.where(block, jnp.where(lane - 8 * s == sub, 1.0, 0.0), panel)
            ahead = s + 1 < STRIPS
            if ahead:
                after = rows[s + 1]
                behind = [
                    jnp.broadcast_to(after[:, 8 * s + j : 8 * s + j + 1], (8, WIDTH))
                    for j in range(8)
                ]
                after = jnp.where(block, 0.0, after)
            pivots = jnp.ones((8, WIDTH), F32)
            for j in range(8):
                pivot = columns[j][j : j + 1]
                inverse = 1.0 / pivot
                pivots = jnp.where(sub == j, pivot, pivots)
                line = panel[j : j + 1]
                if ahead:
                    ratio = behind[j] * inverse
                    after = after - ratio * line
                    for l in range(j + 1, 8):
                        behind[l] = behind[l] - ratio * columns[l][j : j + 1]
                if j < 7:
                    ratio = jnp.where(sub > j, columns[j] * inverse, 0.0)
                    panel = panel - ratio * line
                    for l in range(j + 1, 8):
                        columns[l] = columns[l] - ratio * columns[l][j : j + 1]
            panel = panel * (1.0 / jnp.sqrt(pivots))
            rows[s] = panel
            if ahead:
                rows[s + 1] = after
            if s + 2 < STRIPS:
                a, b, d = [p.astype(F32) for p in pieces(panel, 3)]
                left = jnp.concatenate([a, a, b, b, a, d], axis=0).astype(BF16)
                right = jnp.concatenate([a, b, a, b, d, a], axis=0).astype(BF16)
                change = lax.dot_general(
                    left, right, (((0,), (0,)), ((), ())), preferred_element_type=F32
                )
                for t in range(s + 2, STRIPS):
                    base = jnp.where(block, 0.0, rows[t])
                    rows[t] = base - change[8 * t : 8 * t + 8]
    for g in range(GROUP):
        lower = jnp.concatenate(
            [jnp.where(lane - 8 * s <= sub, strips[g][s], 0.0) for s in range(STRIPS)], axis=0
        )
        upper = lower.T
        slots = pack_strips(
            [upper[8 * s : 8 * s + 8] for s in range(STRIPS)],
            extra_rows(new_means[g], counts[g]),
        )
        for s in range(SLOTS):
            out_ref[g * ROWS + 8 * s : g * ROWS + 8 * s + 8, :] = slots[s]


def solve_share(place, mine, theirs, means):
    smem = pl.BlockSpec(memory_space=pltpu.SMEM)
    vmem = pl.BlockSpec(memory_space=pltpu.VMEM)
    return pl.pallas_call(
        solve_kernel,
        in_specs=[smem, vmem, vmem, vmem],
        out_specs=vmem,
        out_shape=jax.ShapeDtypeStruct((GROUP * ROWS, WIDTH), F32),
        compiler_params=pltpu.CompilerParams(vmem_limit_bytes=VMEM_LIMIT),
        name="solve",
    )(place, mine, theirs, means)


UNPACK = 19


def unpack_kernel(place, here_ref, there_ref, factor_ref, mean_ref, log_ref, counts):
    step = pl.program_id(0)
    for g in range(UNPACK):
        comp = step * UNPACK + g
        half = jnp.where(comp >= HALF, 1, 0)
        at = comp - half * HALF
        q = at // GROUP
        first = pl.multiple_of((at - q * GROUP) * ROWS, 8)
        here = half == place[0]
        slots = []
        for s in range(SLOTS):
            cut = pl.ds(first + 8 * s, 8)
            slots.append(jnp.where(here, here_ref[q, cut, :], there_ref[q, cut, :]))
        strips = unpack_strips(slots)
        for s in range(STRIPS):
            factor_ref[g, 8 * s : 8 * s + 8, :] = strips[s]
        row, count = split_extra(slots[8])
        c = comp // COMPS
        k = comp - c * COMPS
        mean_ref[k, pl.ds(c, 1), :] = row
        counts[k, pl.ds(c, 1), :] = count

    @pl.when(step == CLASSES * COMPS // UNPACK - 1)
    def _():
        mask = iota((CLASSES, WIDTH), 0) == iota((CLASSES, WIDTH), 1)
        values = [counts[k] for k in range(COMPS)]
        total = jnp.log(sum(values) + float(COMPS))
        for k in range(COMPS):
            logs = jnp.where(mask, jnp.log(values[k] + 1.0) - total, 0.0)
            log_ref[k : k + 1, :] = jnp.sum(logs, axis=0, keepdims=True)[:, :CLASSES]


def unpack_all(place, here, there):
    steps = CLASSES * COMPS // UNPACK
    vmem = pl.BlockSpec(memory_space=pltpu.VMEM)
    return pl.pallas_call(
        unpack_kernel,
        grid=(steps,),
        in_specs=[pl.BlockSpec(memory_space=pltpu.SMEM), vmem, vmem],
        out_specs=[
            pl.BlockSpec((UNPACK, WIDTH, WIDTH), lambda i: (i, 0, 0)),
            pl.BlockSpec((COMPS, CLASSES, WIDTH), lambda i: (0, 0, 0)),
            pl.BlockSpec((COMPS, CLASSES), lambda i: (0, 0)),
        ],
        out_shape=[
            jax.ShapeDtypeStruct((CLASSES * COMPS, WIDTH, WIDTH), F32),
            jax.ShapeDtypeStruct((COMPS, CLASSES, WIDTH), F32),
            jax.ShapeDtypeStruct((COMPS, CLASSES), F32),
        ],
        scratch_shapes=[pltpu.VMEM((COMPS, CLASSES, WIDTH), F32)],
        compiler_params=pltpu.CompilerParams(vmem_limit_bytes=VMEM_LIMIT),
        name="unpack",
    )(place, here, there)


def swap_cores(value):
    return lax.ppermute(value, "core", [(0, 1), (1, 0)])


def sum_far(value):
    total = value
    for hop in (2, 1, 3):
        total = total + lax.ppermute(value, "far", [(i, (i + hop) % 4) for i in range(4)])
    return total


def body(embeddings, class_blocks, class_counts, means, log_weights, factors):
    frames_here, pixels_here, width = embeddings.shape
    blocks = embeddings.reshape(frames_here * pixels_here // BLOCK, BLOCK, width)
    core = lax.axis_index("core").astype(jnp.int32)
    late = lax.axis_index("near").astype(jnp.int32)
    owner = (lax.axis_index("x") * 4 + lax.axis_index("y")).astype(jnp.int32)
    means_t = jnp.transpose(means, (1, 0, 2))
    place = core[None]
    own, other = local_moments(
        place, blocks, class_blocks[0, 0].T, class_counts[0, 0], log_weights.T, factors, means_t
    )
    peers = ("x", "y", "near")
    half = own + swap_cores(other)
    parts = lax.all_to_all(half.reshape(2 * OWNERS, PART, width), peers, 0, 0, tiled=True)
    mine = jnp.sum(parts, axis=0)
    mine = sum_far(mine)
    theirs = lax.ppermute(mine, "near", [(0, 1), (1, 0)])
    solved = solve_share(
        jnp.stack([core * HALF + owner * GROUP, late]), mine, theirs, means_t
    )
    spread = jnp.broadcast_to(solved[None], (OWNERS,) + solved.shape)
    here = lax.all_to_all(spread, ("x", "y"), 0, 0, tiled=True)
    there = swap_cores(here)
    new_factor, new_mean, new_log = unpack_all(place, here, there)
    return (
        new_log.T,
        jnp.transpose(new_mean, (1, 0, 2)),
        new_factor.reshape(CLASSES, COMPS, width, width),
    )


def solution(mesh):
    wide = Mesh(mesh.devices.reshape(4, 4, 2, 4, 2), ("x", "far", "near", "y", "core"))
    space = ("far", "near", "y", "core")
    return jax.shard_map(
        body,
        mesh=wide,
        in_specs=(P("x", space, None), P("x", space, None, None), P("x", space, None), P(), P(), P()),
        out_specs=(P(), P(), P()),
        check_vma=False,
    )
```

```python
import functools
import jax
import jax.numpy as jnp
from jax import lax
from jax.experimental import pallas as pl
from jax.experimental.pallas import tpu as pltpu
from jax.sharding import Mesh, PartitionSpec as P

CLASSES = 19
COMPS = 5
WIDTH = 128
BLOCK = 128
ROWS = 72
STRIPS = 16
F32 = jnp.float32
BF16 = jnp.bfloat16
SLOTS = 9
GROUP = 3
UNROLL = 2
OWNERS = 16
HALF = GROUP * OWNERS
SHARE = 224
PART = SHARE // 2
VMEM_LIMIT = 48 * 1024 * 1024


def iota(shape, axis):
    return lax.broadcasted_iota(jnp.int32, shape, axis)


def pieces(value, count):
    out = []
    for _ in range(count):
        part = value.astype(BF16)
        out.append(part)
        value = value - part.astype(F32)
    return out


def pack_strips(strips, extra):
    lane = iota((8, WIDTH), 1)
    out = [strips[0]]
    for s in range(1, 8):
        moved = pltpu.roll(strips[16 - s], 8 * s, 1)
        out.append(jnp.where(lane >= 8 * s, strips[s], moved))
    out.append(jnp.where(lane >= 64, strips[8], extra))
    return out


def unpack_strips(slots):
    lane = iota((8, WIDTH), 1)
    strips = [None] * 16
    strips[0] = slots[0]
    for s in range(1, 8):
        strips[s] = jnp.where(lane >= 8 * s, slots[s], 0.0)
        moved = pltpu.roll(slots[s], WIDTH - 8 * s, 1)
        strips[16 - s] = jnp.where(lane >= WIDTH - 8 * s, moved, 0.0)
    strips[8] = jnp.where(lane >= 64, slots[8], 0.0)
    return strips


def extra_rows(row, count):
    sub = iota((8, WIDTH), 0)
    later = pltpu.roll(jnp.broadcast_to(row, (8, WIDTH)), 64, 1)
    return jnp.where(sub == 0, row, jnp.where(sub == 1, later, jnp.where(sub == 2, count, 0.0)))


def split_extra(slot):
    lane = iota((8, WIDTH), 1)
    moved = pltpu.roll(slot, 64, 1)
    row = jnp.where(lane[0:1] < 64, slot[0:1], moved[1:2])
    count = jnp.where(lane[0:1] < 64, slot[2:3], moved[2:3])
    return row, count


def moments_kernel(place, lists_any, counts_any, lw_any, emb_any, fac_any, mean_any, own_ref, other_ref,
                   acc, tot, cnt, flipped, shift, const, rows_t, gate, items,
                   lists, list_counts, lw_ref, emb_ref, fac_ref, mean_ref, sems):
    pairs = ((lists_any, lists), (counts_any, list_counts), (lw_any, lw_ref), (emb_any, emb_ref),
             (fac_any, fac_ref), (mean_any, mean_ref))
    copies = [pltpu.make_async_copy(src, dst, sems.at[n]) for n, (src, dst) in enumerate(pairs)]
    for copy in copies:
        copy.start()
    sub = iota((8, WIDTH), 0)
    lane = iota((8, WIDTH), 1)
    ident = (iota((WIDTH, WIDTH), 0) == iota((WIDTH, WIDTH), 1)).astype(F32).astype(BF16)

    acc[...] = jnp.zeros_like(acc)
    tot[...] = jnp.zeros_like(tot)
    cnt[...] = jnp.zeros_like(cnt)
    gate[...] = jnp.zeros_like(gate)
    rows_t[...] = jnp.zeros_like(rows_t)

    copies[0].wait()
    copies[1].wait()

    def list_class(c, at):
        n = list_counts[c]

        def list_pair(t, at):
            items[0, at] = c
            items[1, at] = lists[2 * t, c]
            items[2, at] = lists[2 * t + 1, c]
            items[3, at] = jnp.where(2 * t + 1 < n, 2 * BLOCK, BLOCK)
            return at + 1

        return lax.fori_loop(0, (n + 1) // 2, list_pair, at)

    total_items = lax.fori_loop(0, CLASSES, list_class, jnp.int32(0))

    for copy in copies[2:]:
        copy.wait()

    def clamp(i):
        return jnp.minimum(jnp.maximum(i, 0), total_items - 1)

    def moments_of(i, u):
        at = clamp(i)
        c = items[0, at]
        rows = jnp.concatenate([emb_ref[items[1, at]], emb_ref[items[2, at]]], axis=0)
        weights = gate[u]
        flat = rows_t[u]
        both = jnp.concatenate([rows, rows], axis=0)
        for k in range(COMPS):
            high, low = pieces(flat * weights[k : k + 1], 2)
            acc[c * COMPS + k] += jnp.dot(
                jnp.concatenate([high, low], axis=1), both, preferred_element_type=F32
            )
        tall = jnp.concatenate([weights, jnp.zeros_like(weights)])
        sums = jnp.dot(jnp.concatenate(pieces(tall, 3)), rows, preferred_element_type=F32)
        tot[c] += sums[0:8] + sums[16:24] + sums[32:40]
        cnt[c] += weights[:, :BLOCK] + weights[:, BLOCK:]

    def scores_of(i, u):
        at = clamp(i)
        first = emb_ref[items[1, at]].astype(F32).T
        later = emb_ref[items[2, at]].astype(F32).T
        flat = jnp.concatenate([first, later], axis=1)
        square = jnp.zeros((8, 2 * BLOCK), F32)
        wide_sub = iota((8, 2 * BLOCK), 0)
        flat_half = flat.astype(BF16)
        offsets = shift[u].astype(BF16)
        row = iota((WIDTH, 2 * BLOCK), 0)
        for k in range(COMPS):
            ones = jnp.where((row >= 3 * k) & (row < 3 * k + 3), 1.0, 0.0).astype(BF16)
            centred = jnp.dot(
                jnp.concatenate([flipped[u, k], offsets], axis=1),
                jnp.concatenate([flat_half, ones], axis=0),
                preferred_element_type=F32,
            )
            line = jnp.sum(centred * centred, axis=0, keepdims=True)
            square = jnp.where(wide_sub == k, line, square)
        consts = const[u]
        scores = jnp.concatenate([consts, consts], axis=1) - 0.5 * square
        top = jnp.max(scores, axis=0, keepdims=True)
        weights = jnp.exp(scores - top)
        weights = weights / jnp.sum(weights, axis=0, keepdims=True)
        live = jnp.where((i >= 0) & (i < total_items), items[3, at], 0)
        gate[u] = jnp.where(iota((8, 2 * BLOCK), 1) < live, weights, 0.0)
        rows_t[u] = flat

    def prepare(i, u):
        c = items[0, clamp(i)]
        diag = jnp.ones((8, WIDTH), F32)
        prior = jnp.full((8, WIDTH), -1e30, F32)
        mean = mean_ref[:, c]
        mean_pieces = jnp.concatenate(
            pieces(jnp.concatenate([mean, jnp.zeros((16 - COMPS, WIDTH), F32)]), 3)
        )
        lines = []
        for k in range(COMPS):
            factor = fac_ref[c, k]
            wide = factor.astype(F32)
            on_diag = None
            for s in range(STRIPS):
                part = jnp.where(lane - 8 * s == sub, wide[8 * s : 8 * s + 8], 0.0)
                on_diag = part if on_diag is None else on_diag + part
            diag = jnp.where(sub == k, jnp.sum(on_diag, axis=0, keepdims=True), diag)
            prior = jnp.where(sub == k, lw_ref[k, c], prior)
            flipped[u, k] = wide.T.astype(BF16)
            parts = jnp.dot(mean_pieces, factor, preferred_element_type=F32)
            line = parts[k : k + 1] + parts[16 + k : 17 + k] + parts[32 + k : 33 + k]
            lines += [-p.astype(F32) for p in pieces(line, 3)]
        shift[u] = jnp.concatenate(lines + [jnp.zeros((WIDTH - 3 * COMPS, WIDTH), F32)], axis=0).T
        const[u] = jnp.sum(jnp.log(diag), axis=1, keepdims=True) + prior

    def step(j, carry):
        for u in range(UNROLL):
            moments_of(UNROLL * (j - 2) + u, u)
        for u in range(UNROLL):
            scores_of(UNROLL * (j - 1) + u, u)
        for u in range(UNROLL):
            prepare(UNROLL * j + u, u)
        return carry

    lax.fori_loop(0, (total_items + UNROLL - 1) // UNROLL + 2, step, 0)

    def pack(q, carry):
        for base, out_ref in ((place[0], own_ref), (1 - place[0], other_ref)):
            for r in range(GROUP):
                slot = base * HALF + q * GROUP + r
                c = slot // COMPS
                k = slot - c * COMPS
                counted = cnt[c, pl.ds(k, 1), :]
                count = jnp.broadcast_to(jnp.sum(counted, axis=1, keepdims=True), (1, WIDTH))
                slots = pack_strips(
                    [acc[slot, 8 * s : 8 * s + 8, :] for s in range(STRIPS)],
                    extra_rows(tot[c, pl.ds(k, 1), :], count),
                )
                for s in range(SLOTS):
                    out_ref[q, r * ROWS + 8 * s : r * ROWS + 8 * s + 8, :] = slots[s]
            out_ref[q, GROUP * ROWS : SHARE, :] = jnp.zeros((SHARE - GROUP * ROWS, WIDTH), F32)
        return carry

    lax.fori_loop(0, OWNERS, pack, 0)


def local_moments(place, blocks, lists, list_counts, log_weights, factors, means):
    vmem = pl.BlockSpec(memory_space=pltpu.VMEM)
    smem = pl.BlockSpec(memory_space=pltpu.SMEM)
    anywhere = pl.BlockSpec(memory_space=pltpu.HBM)
    return pl.pallas_call(
        moments_kernel,
        in_specs=[smem] + [anywhere] * 6,
        out_specs=[vmem, vmem],
        scratch_shapes=[
            pltpu.VMEM(((CLASSES + 1) * COMPS, WIDTH, WIDTH), F32),
            pltpu.VMEM((CLASSES + 1, 8, WIDTH), F32),
            pltpu.VMEM((CLASSES + 1, 8, WIDTH), F32),
            pltpu.VMEM((UNROLL, COMPS, WIDTH, WIDTH), BF16),
            pltpu.VMEM((UNROLL, WIDTH, WIDTH), F32),
            pltpu.VMEM((UNROLL, 8, WIDTH), F32),
            pltpu.VMEM((UNROLL, WIDTH, 2 * BLOCK), F32),
            pltpu.VMEM((UNROLL, 8, 2 * BLOCK), F32),
            pltpu.SMEM((4, 128), jnp.int32),
            pltpu.SMEM(lists.shape, jnp.int32),
            pltpu.SMEM(list_counts.shape, jnp.int32),
            pltpu.SMEM(log_weights.shape, F32),
            pltpu.VMEM(blocks.shape, BF16),
            pltpu.VMEM(factors.shape, BF16),
            pltpu.VMEM(means.shape, F32),
            pltpu.SemaphoreType.DMA((6,)),
        ],
        out_shape=[jax.ShapeDtypeStruct((OWNERS, SHARE, WIDTH), F32)] * 2,
        compiler_params=pltpu.CompilerParams(vmem_limit_bytes=VMEM_LIMIT),
        name="moments",
    )(place, *[pltpu.with_memory_space_constraint(v, pltpu.HBM) for v in (lists, list_counts, log_weights, blocks, factors, means)])


def solve_kernel(place, mine_ref, theirs_ref, mean_ref, out_ref):
    lane = iota((8, WIDTH), 1)
    sub = iota((8, WIDTH), 0)
    early = place[1] == 0
    share = []
    for at in range(2):
        for t in range(PART // 8):
            cut = slice(8 * t, 8 * t + 8)
            share.append(jnp.where(early == (at == 0), mine_ref[cut, :], theirs_ref[cut, :]))
    strips, new_means, counts = [], [], []
    for g in range(GROUP):
        slots = share[SLOTS * g : SLOTS * g + SLOTS]
        totals, count = split_extra(slots[8])
        comp = jnp.minimum(place[0] + g, CLASSES * COMPS - 1)
        old = mean_ref[lax.rem(comp, COMPS), pl.ds(comp // COMPS, 1), :]
        denom = count + 1.0
        new = (totals + old) / denom
        old_t = jnp.broadcast_to(old, (WIDTH, WIDTH)).T
        new_t = jnp.broadcast_to(new * denom, (WIDTH, WIDTH)).T
        second = unpack_strips(slots)
        full = jnp.concatenate(second, axis=0)
        mirror = full.T
        rows = []
        for s in range(STRIPS):
            cut = slice(8 * s, 8 * s + 8)
            scatter = jnp.where(lane >= 8 * s, second[s], mirror[cut])
            scatter = scatter + old_t[cut] * old - new_t[cut] * new
            scatter = jnp.where(lane - 8 * s == sub, scatter + 1.0, scatter)
            rows.append(scatter / denom)
        strips.append(rows)
        new_means.append(new)
        counts.append(count)
    for s in range(STRIPS):
        for g in range(GROUP):
            rows = strips[g]
            block = (lane >= 8 * s) & (lane < 8 * s + 8)
            panel = rows[s]
            columns = [
                jnp.broadcast_to(panel[:, 8 * s + j : 8 * s + j + 1], (8, WIDTH)) for j in range(8)
            ]
            panel = jnp.where(block, jnp.where(lane - 8 * s == sub, 1.0, 0.0), panel)
            ahead = s + 1 < STRIPS
            if ahead:
                after = rows[s + 1]
                behind = [
                    jnp.broadcast_to(after[:, 8 * s + j : 8 * s + j + 1], (8, WIDTH))
                    for j in range(8)
                ]
                after = jnp.where(block, 0.0, after)
            pivots = jnp.ones((8, WIDTH), F32)
            for j in range(8):
                pivot = columns[j][j : j + 1]
                inverse = 1.0 / pivot
                pivots = jnp.where(sub == j, pivot, pivots)
                line = panel[j : j + 1]
                if ahead:
                    ratio = behind[j] * inverse
                    after = after - ratio * line
                    for l in range(j + 1, 8):
                        behind[l] = behind[l] - ratio * columns[l][j : j + 1]
                if j < 7:
                    ratio = jnp.where(sub > j, columns[j] * inverse, 0.0)
                    panel = panel - ratio * line
                    for l in range(j + 1, 8):
                        columns[l] = columns[l] - ratio * columns[l][j : j + 1]
            panel = panel * (1.0 / jnp.sqrt(pivots))
            rows[s] = panel
            if ahead:
                rows[s + 1] = after
            if s + 2 < STRIPS:
                a, b, d = [p.astype(F32) for p in pieces(panel, 3)]
                left = jnp.concatenate([a, a, b, b, a, d], axis=0).astype(BF16)
                right = jnp.concatenate([a, b, a, b, d, a], axis=0).astype(BF16)
                change = lax.dot_general(
                    left, right, (((0,), (0,)), ((), ())), preferred_element_type=F32
                )
                for t in range(s + 2, STRIPS):
                    base = jnp.where(block, 0.0, rows[t])
                    rows[t] = base - change[8 * t : 8 * t + 8]
    for g in range(GROUP):
        lower = jnp.concatenate(
            [jnp.where(lane - 8 * s <= sub, strips[g][s], 0.0) for s in range(STRIPS)], axis=0
        )
        upper = lower.T
        slots = pack_strips(
            [upper[8 * s : 8 * s + 8] for s in range(STRIPS)],
            extra_rows(new_means[g], counts[g]),
        )
        for s in range(SLOTS):
            out_ref[g * ROWS + 8 * s : g * ROWS + 8 * s + 8, :] = slots[s]


def solve_share(place, mine, theirs, means):
    smem = pl.BlockSpec(memory_space=pltpu.SMEM)
    vmem = pl.BlockSpec(memory_space=pltpu.VMEM)
    return pl.pallas_call(
        solve_kernel,
        in_specs=[smem, vmem, vmem, vmem],
        out_specs=vmem,
        out_shape=jax.ShapeDtypeStruct((GROUP * ROWS, WIDTH), F32),
        compiler_params=pltpu.CompilerParams(vmem_limit_bytes=VMEM_LIMIT),
        name="solve",
    )(place, mine, theirs, means)


def unpack_half(half, part_ref, factor_any, mean_ref, counts, buffer, sems):
    def copy_of(at):
        comp = half * HALF + at
        copy = pltpu.make_async_copy(buffer.at[at], factor_any.at[comp], sems.at[at])
        return comp < CLASSES * COMPS, copy

    def unpack(q, carry):
        for r in range(GROUP):
            at = q * GROUP + r
            comp = half * HALF + at
            slots = [part_ref[q, r * ROWS + 8 * s : r * ROWS + 8 * s + 8, :] for s in range(SLOTS)]
            strips = unpack_strips(slots)
            for s in range(STRIPS):
                buffer[at, 8 * s : 8 * s + 8, :] = strips[s]
            row, count = split_extra(slots[8])
            c = jnp.minimum(comp // COMPS, CLASSES)
            k = comp - comp // COMPS * COMPS
            mean_ref[k, pl.ds(c, 1), :] = row
            counts[k, pl.ds(c, 1), :] = count
        for r in range(GROUP):
            real, copy = copy_of(q * GROUP + r)
            pl.when(real)(copy.start)
        return carry

    def finish(at, carry):
        real, copy = copy_of(at)
        pl.when(real)(copy.wait)
        return carry

    lax.fori_loop(0, OWNERS, unpack, 0)
    return finish


def unpack_first_kernel(place, part_ref, factor_any, mean_ref, count_ref, buffer, sems):
    finish = unpack_half(place[0], part_ref, factor_any, mean_ref, count_ref, buffer, sems)
    lax.fori_loop(0, HALF, finish, 0)


def unpack_last_kernel(place, part_ref, begun_any, mean_part, count_part, factor_any, mean_ref, log_ref,
                       means, counts, buffer, sems):
    half = 1 - place[0]
    finish = unpack_half(half, part_ref, factor_any, means, counts, buffer, sems)
    comp = iota((PADDED, WIDTH), 0) * COMPS
    values = []
    for k in range(COMPS):
        here = (comp + k >= HALF) == (half == 1)
        mean_ref[k] = jnp.where(here, means[k], mean_part[k])[:CLASSES]
        values.append(jnp.where(here, counts[k], count_part[k])[:CLASSES])
    mask = iota((CLASSES, WIDTH), 0) == iota((CLASSES, WIDTH), 1)
    total = jnp.log(sum(values) + float(COMPS))
    for k in range(COMPS):
        logs = jnp.where(mask, jnp.log(values[k] + 1.0) - total, 0.0)
        log_ref[k : k + 1, :] = jnp.sum(logs, axis=0, keepdims=True)[:, :CLASSES]
    lax.fori_loop(0, HALF, finish, 0)


PADDED = 24


def unpack_all(place, here, there_of):
    vmem = pl.BlockSpec(memory_space=pltpu.VMEM)
    smem = pl.BlockSpec(memory_space=pltpu.SMEM)
    hbm = pl.BlockSpec(memory_space=pltpu.HBM)
    factor = jax.ShapeDtypeStruct((CLASSES * COMPS, WIDTH, WIDTH), F32)
    part = jax.ShapeDtypeStruct((COMPS, PADDED, WIDTH), F32)
    work = [pltpu.VMEM((HALF, WIDTH, WIDTH), F32), pltpu.SemaphoreType.DMA((HALF,))]
    rows = pltpu.VMEM(part.shape, F32)
    cost = pl.CostEstimate(flops=4000000, bytes_accessed=5000000, transcendentals=0)
    params = pltpu.CompilerParams(vmem_limit_bytes=VMEM_LIMIT)
    there = there_of(here)
    begun, mean_part, count_part = pl.pallas_call(
        unpack_first_kernel,
        in_specs=[smem, vmem],
        out_specs=[hbm, vmem, vmem],
        out_shape=[factor, part, part],
        scratch_shapes=work,
        compiler_params=params,
        cost_estimate=cost,
        name="unpack_first",
    )(place, here)
    return pl.pallas_call(
        unpack_last_kernel,
        in_specs=[smem, vmem, hbm, vmem, vmem],
        out_specs=[hbm, vmem, vmem],
        out_shape=[
            factor,
            jax.ShapeDtypeStruct((COMPS, CLASSES, WIDTH), F32),
            jax.ShapeDtypeStruct((COMPS, CLASSES), F32),
        ],
        input_output_aliases={2: 0},
        scratch_shapes=[rows, rows] + work,
        compiler_params=params,
        cost_estimate=cost,
        name="unpack_last",
    )(place, there, begun, mean_part, count_part)


def swap_cores(value):
    return lax.ppermute(value, "core", [(0, 1), (1, 0)])


def sum_far(value):
    total = value
    for hop in (2, 1, 3):
        total = total + lax.ppermute(value, "far", [(i, (i + hop) % 4) for i in range(4)])
    return total


def body(embeddings, class_blocks, class_counts, means, log_weights, factors):
    frames_here, pixels_here, width = embeddings.shape
    blocks = embeddings.reshape(frames_here * pixels_here // BLOCK, BLOCK, width)
    core = lax.axis_index("core").astype(jnp.int32)
    late = lax.axis_index("near").astype(jnp.int32)
    owner = (lax.axis_index("x") * 4 + lax.axis_index("y")).astype(jnp.int32)
    means_t = jnp.transpose(means, (1, 0, 2))
    place = core[None]
    own, other = local_moments(
        place, blocks, class_blocks[0, 0].T, class_counts[0, 0], log_weights.T, factors, means_t
    )
    peers = ("x", "y", "near")
    half = own + swap_cores(other)
    parts = lax.all_to_all(half.reshape(2 * OWNERS, PART, width), peers, 0, 0, tiled=True)
    mine = jnp.sum(parts, axis=0)
    mine = sum_far(mine)
    theirs = lax.ppermute(mine, "near", [(0, 1), (1, 0)])
    solved = solve_share(
        jnp.stack([core * HALF + owner * GROUP, late]), mine, theirs, means_t
    )
    spread = jnp.broadcast_to(solved[None], (OWNERS,) + solved.shape)
    here = lax.all_to_all(spread, ("x", "y"), 0, 0, tiled=True)
    new_factor, new_mean, new_log = unpack_all(place, here, swap_cores)
    return (
        new_log.T,
        jnp.transpose(new_mean, (1, 0, 2)),
        new_factor.reshape(CLASSES, COMPS, width, width),
    )


def solution(mesh):
    wide = Mesh(mesh.devices.reshape(4, 4, 2, 4, 2), ("x", "far", "near", "y", "core"))
    space = ("far", "near", "y", "core")
    return jax.shard_map(
        body,
        mesh=wide,
        in_specs=(P("x", space, None), P("x", space, None, None), P("x", space, None), P(), P(), P()),
        out_specs=(P(), P(), P()),
        check_vma=False,
    )
```

```python
import functools
import jax
import jax.numpy as jnp
from jax import lax
from jax.experimental import pallas as pl
from jax.experimental.pallas import tpu as pltpu
from jax.sharding import Mesh, PartitionSpec as P

CLASSES = 19
COMPS = 5
WIDTH = 128
BLOCK = 128
ROWS = 72
STRIPS = 16
F32 = jnp.float32
BF16 = jnp.bfloat16
SLOTS = 9
GROUP = 3
UNROLL = 3
OWNERS = 16
HALF = GROUP * OWNERS
SHARE = 224
PART = SHARE // 2
VMEM_LIMIT = 48 * 1024 * 1024


def iota(shape, axis):
    return lax.broadcasted_iota(jnp.int32, shape, axis)


def pieces(value, count):
    out = []
    for _ in range(count):
        part = value.astype(BF16)
        out.append(part)
        value = value - part.astype(F32)
    return out


def pack_strips(strips, extra):
    lane = iota((8, WIDTH), 1)
    out = [strips[0]]
    for s in range(1, 8):
        moved = pltpu.roll(strips[16 - s], 8 * s, 1)
        out.append(jnp.where(lane >= 8 * s, strips[s], moved))
    out.append(jnp.where(lane >= 64, strips[8], extra))
    return out


def unpack_strips(slots):
    lane = iota((8, WIDTH), 1)
    strips = [None] * 16
    strips[0] = slots[0]
    for s in range(1, 8):
        strips[s] = jnp.where(lane >= 8 * s, slots[s], 0.0)
        moved = pltpu.roll(slots[s], WIDTH - 8 * s, 1)
        strips[16 - s] = jnp.where(lane >= WIDTH - 8 * s, moved, 0.0)
    strips[8] = jnp.where(lane >= 64, slots[8], 0.0)
    return strips


def extra_rows(row, count):
    sub = iota((8, WIDTH), 0)
    later = pltpu.roll(jnp.broadcast_to(row, (8, WIDTH)), 64, 1)
    return jnp.where(sub == 0, row, jnp.where(sub == 1, later, jnp.where(sub == 2, count, 0.0)))


def split_extra(slot):
    lane = iota((8, WIDTH), 1)
    moved = pltpu.roll(slot, 64, 1)
    row = jnp.where(lane[0:1] < 64, slot[0:1], moved[1:2])
    count = jnp.where(lane[0:1] < 64, slot[2:3], moved[2:3])
    return row, count


def moments_kernel(place, lists_any, counts_any, lw_any, emb_any, fac_any, mean_any, own_ref, other_ref,
                   acc, tot, cnt, flipped, shift, const, rows_t, gate, items,
                   lists, list_counts, lw_ref, emb_ref, fac_ref, mean_ref, sems):
    pairs = ((lists_any, lists), (counts_any, list_counts), (lw_any, lw_ref), (emb_any, emb_ref),
             (fac_any, fac_ref), (mean_any, mean_ref))
    copies = [pltpu.make_async_copy(src, dst, sems.at[n]) for n, (src, dst) in enumerate(pairs)]
    for copy in copies:
        copy.start()
    sub = iota((8, WIDTH), 0)
    lane = iota((8, WIDTH), 1)
    ident = (iota((WIDTH, WIDTH), 0) == iota((WIDTH, WIDTH), 1)).astype(F32).astype(BF16)

    acc[...] = jnp.zeros_like(acc)
    tot[...] = jnp.zeros_like(tot)
    cnt[...] = jnp.zeros_like(cnt)

    copies[0].wait()
    copies[1].wait()

    def list_class(c, at):
        n = list_counts[c]

        def list_pair(t, at):
            items[0, at] = c
            items[1, at] = lists[2 * t, c]
            items[2, at] = lists[2 * t + 1, c]
            items[3, at] = jnp.where(2 * t + 1 < n, 2 * BLOCK, BLOCK)
            return at + 1

        return lax.fori_loop(0, (n + 1) // 2, list_pair, at)

    total_items = lax.fori_loop(0, CLASSES, list_class, jnp.int32(0))

    for copy in copies[2:]:
        copy.wait()

    def clamp(i):
        return jnp.minimum(jnp.maximum(i, 0), total_items - 1)

    def moments_of(i, u):
        at = clamp(i)
        c = items[0, at]
        rows = jnp.concatenate([emb_ref[items[1, at]], emb_ref[items[2, at]]], axis=0)
        weights = gate[u]
        flat = rows_t[u]
        both = jnp.concatenate([rows, rows], axis=0)
        for k in range(COMPS):
            high, low = pieces(flat * weights[k : k + 1], 2)
            acc[c * COMPS + k] += jnp.dot(
                jnp.concatenate([high, low], axis=1), both, preferred_element_type=F32
            )
        tall = jnp.concatenate([weights, jnp.zeros_like(weights)])
        sums = jnp.dot(jnp.concatenate(pieces(tall, 3)), rows, preferred_element_type=F32)
        tot[c] += sums[0:8] + sums[16:24] + sums[32:40]
        cnt[c] += weights[:, :BLOCK] + weights[:, BLOCK:]

    def scores_of(i, u):
        at = clamp(i)
        first = emb_ref[items[1, at]].astype(F32).T
        later = emb_ref[items[2, at]].astype(F32).T
        flat = jnp.concatenate([first, later], axis=1)
        square = jnp.zeros((8, 2 * BLOCK), F32)
        wide_sub = iota((8, 2 * BLOCK), 0)
        flat_half = flat.astype(BF16)
        offsets = shift[u].astype(BF16)
        row = iota((WIDTH, 2 * BLOCK), 0)
        for k in range(COMPS):
            ones = jnp.where((row >= 3 * k) & (row < 3 * k + 3), 1.0, 0.0).astype(BF16)
            centred = jnp.dot(
                jnp.concatenate([flipped[u, k], offsets], axis=1),
                jnp.concatenate([flat_half, ones], axis=0),
                preferred_element_type=F32,
            )
            line = jnp.sum(centred * centred, axis=0, keepdims=True)
            square = jnp.where(wide_sub == k, line, square)
        consts = const[u]
        scores = jnp.concatenate([consts, consts], axis=1) - 0.5 * square
        top = jnp.max(scores, axis=0, keepdims=True)
        weights = jnp.exp(scores - top)
        weights = weights / jnp.sum(weights, axis=0, keepdims=True)
        live = jnp.where((i >= 0) & (i < total_items), items[3, at], 0)
        gate[u] = jnp.where(iota((8, 2 * BLOCK), 1) < live, weights, 0.0)
        rows_t[u] = flat

    def prepare(i, u):
        c = items[0, clamp(i)]
        diag = jnp.ones((8, WIDTH), F32)
        prior = jnp.full((8, WIDTH), -1e30, F32)
        mean = mean_ref[:, c]
        mean_pieces = jnp.concatenate(
            pieces(jnp.concatenate([mean, jnp.zeros((16 - COMPS, WIDTH), F32)]), 3)
        )
        lines = []
        for k in range(COMPS):
            factor = fac_ref[c, k]
            wide = factor.astype(F32)
            on_diag = None
            for s in range(STRIPS):
                part = jnp.where(lane - 8 * s == sub, wide[8 * s : 8 * s + 8], 0.0)
                on_diag = part if on_diag is None else on_diag + part
            diag = jnp.where(sub == k, jnp.sum(on_diag, axis=0, keepdims=True), diag)
            prior = jnp.where(sub == k, lw_ref[k, c], prior)
            flipped[u, k] = wide.T.astype(BF16)
            parts = jnp.dot(mean_pieces, factor, preferred_element_type=F32)
            line = parts[k : k + 1] + parts[16 + k : 17 + k] + parts[32 + k : 33 + k]
            lines += [-p.astype(F32) for p in pieces(line, 3)]
        shift[u] = jnp.concatenate(lines + [jnp.zeros((WIDTH - 3 * COMPS, WIDTH), F32)], axis=0).T
        const[u] = jnp.sum(jnp.log(diag), axis=1, keepdims=True) + prior

    def stage(work, j):
        for u in range(UNROLL):
            work(UNROLL * j + u, u)

    def step(j, carry):
        stage(moments_of, j - 2)
        stage(scores_of, j - 1)
        stage(prepare, j)
        return carry

    groups = (total_items + UNROLL - 1) // UNROLL
    stage(prepare, 0)
    stage(scores_of, 0)
    stage(prepare, 1)
    lax.fori_loop(2, groups, step, 0)
    stage(moments_of, jnp.maximum(groups - 2, 0))
    stage(scores_of, groups - 1)
    stage(moments_of, groups - 1)

    def pack(q, carry):
        for base, out_ref in ((place[0], own_ref), (1 - place[0], other_ref)):
            for r in range(GROUP):
                slot = base * HALF + q * GROUP + r
                c = slot // COMPS
                k = slot - c * COMPS
                counted = cnt[c, pl.ds(k, 1), :]
                count = jnp.broadcast_to(jnp.sum(counted, axis=1, keepdims=True), (1, WIDTH))
                slots = pack_strips(
                    [acc[slot, 8 * s : 8 * s + 8, :] for s in range(STRIPS)],
                    extra_rows(tot[c, pl.ds(k, 1), :], count),
                )
                for s in range(SLOTS):
                    out_ref[q, r * ROWS + 8 * s : r * ROWS + 8 * s + 8, :] = slots[s]
            out_ref[q, GROUP * ROWS : SHARE, :] = jnp.zeros((SHARE - GROUP * ROWS, WIDTH), F32)
        return carry

    lax.fori_loop(0, OWNERS, pack, 0)


def local_moments(place, blocks, lists, list_counts, log_weights, factors, means):
    vmem = pl.BlockSpec(memory_space=pltpu.VMEM)
    smem = pl.BlockSpec(memory_space=pltpu.SMEM)
    anywhere = pl.BlockSpec(memory_space=pltpu.HBM)
    return pl.pallas_call(
        moments_kernel,
        in_specs=[smem] + [anywhere] * 6,
        out_specs=[vmem, vmem],
        scratch_shapes=[
            pltpu.VMEM(((CLASSES + 1) * COMPS, WIDTH, WIDTH), F32),
            pltpu.VMEM((CLASSES + 1, 8, WIDTH), F32),
            pltpu.VMEM((CLASSES + 1, 8, WIDTH), F32),
            pltpu.VMEM((UNROLL, COMPS, WIDTH, WIDTH), BF16),
            pltpu.VMEM((UNROLL, WIDTH, WIDTH), F32),
            pltpu.VMEM((UNROLL, 8, WIDTH), F32),
            pltpu.VMEM((UNROLL, WIDTH, 2 * BLOCK), F32),
            pltpu.VMEM((UNROLL, 8, 2 * BLOCK), F32),
            pltpu.SMEM((4, 128), jnp.int32),
            pltpu.SMEM(lists.shape, jnp.int32),
            pltpu.SMEM(list_counts.shape, jnp.int32),
            pltpu.SMEM(log_weights.shape, F32),
            pltpu.VMEM(blocks.shape, BF16),
            pltpu.VMEM(factors.shape, BF16),
            pltpu.VMEM(means.shape, F32),
            pltpu.SemaphoreType.DMA((6,)),
        ],
        out_shape=[jax.ShapeDtypeStruct((OWNERS, SHARE, WIDTH), F32)] * 2,
        compiler_params=pltpu.CompilerParams(vmem_limit_bytes=VMEM_LIMIT),
        name="moments",
    )(place, *[pltpu.with_memory_space_constraint(v, pltpu.HBM) for v in (lists, list_counts, log_weights, blocks, factors, means)])


def solve_kernel(place, mine_ref, theirs_ref, mean_ref, out_ref):
    lane = iota((8, WIDTH), 1)
    sub = iota((8, WIDTH), 0)
    early = place[1] == 0
    share = []
    for at in range(2):
        for t in range(PART // 8):
            cut = slice(8 * t, 8 * t + 8)
            share.append(jnp.where(early == (at == 0), mine_ref[cut, :], theirs_ref[cut, :]))
    strips, new_means, counts = [], [], []
    for g in range(GROUP):
        slots = share[SLOTS * g : SLOTS * g + SLOTS]
        totals, count = split_extra(slots[8])
        comp = jnp.minimum(place[0] + g, CLASSES * COMPS - 1)
        old = mean_ref[lax.rem(comp, COMPS), pl.ds(comp // COMPS, 1), :]
        denom = count + 1.0
        new = (totals + old) / denom
        old_t = jnp.broadcast_to(old, (WIDTH, WIDTH)).T
        new_t = jnp.broadcast_to(new * denom, (WIDTH, WIDTH)).T
        second = unpack_strips(slots)
        full = jnp.concatenate(second, axis=0)
        mirror = full.T
        rows = []
        for s in range(STRIPS):
            cut = slice(8 * s, 8 * s + 8)
            scatter = jnp.where(lane >= 8 * s, second[s], mirror[cut])
            scatter = scatter + old_t[cut] * old - new_t[cut] * new
            scatter = jnp.where(lane - 8 * s == sub, scatter + 1.0, scatter)
            rows.append(scatter / denom)
        strips.append(rows)
        new_means.append(new)
        counts.append(count)
    for s in range(STRIPS):
        for g in range(GROUP):
            rows = strips[g]
            block = (lane >= 8 * s) & (lane < 8 * s + 8)
            panel = rows[s]
            columns = [
                jnp.broadcast_to(panel[:, 8 * s + j : 8 * s + j + 1], (8, WIDTH)) for j in range(8)
            ]
            panel = jnp.where(block, jnp.where(lane - 8 * s == sub, 1.0, 0.0), panel)
            ahead = s + 1 < STRIPS
            if ahead:
                after = rows[s + 1]
                behind = [
                    jnp.broadcast_to(after[:, 8 * s + j : 8 * s + j + 1], (8, WIDTH))
                    for j in range(8)
                ]
                after = jnp.where(block, 0.0, after)
            pivots = jnp.ones((8, WIDTH), F32)
            for j in range(8):
                pivot = columns[j][j : j + 1]
                inverse = 1.0 / pivot
                pivots = jnp.where(sub == j, pivot, pivots)
                line = panel[j : j + 1]
                if ahead:
                    ratio = behind[j] * inverse
                    after = after - ratio * line
                    for l in range(j + 1, 8):
                        behind[l] = behind[l] - ratio * columns[l][j : j + 1]
                if j < 7:
                    ratio = jnp.where(sub > j, columns[j] * inverse, 0.0)
                    panel = panel - ratio * line
                    for l in range(j + 1, 8):
                        columns[l] = columns[l] - ratio * columns[l][j : j + 1]
            panel = panel * (1.0 / jnp.sqrt(pivots))
            rows[s] = panel
            if ahead:
                rows[s + 1] = after
            if s + 2 < STRIPS:
                a, b, d = [p.astype(F32) for p in pieces(panel, 3)]
                left = jnp.concatenate([a, a, b, b, a, d], axis=0).astype(BF16)
                right = jnp.concatenate([a, b, a, b, d, a], axis=0).astype(BF16)
                change = lax.dot_general(
                    left, right, (((0,), (0,)), ((), ())), preferred_element_type=F32
                )
                for t in range(s + 2, STRIPS):
                    base = jnp.where(block, 0.0, rows[t])
                    rows[t] = base - change[8 * t : 8 * t + 8]
    for g in range(GROUP):
        lower = jnp.concatenate(
            [jnp.where(lane - 8 * s <= sub, strips[g][s], 0.0) for s in range(STRIPS)], axis=0
        )
        upper = lower.T
        slots = pack_strips(
            [upper[8 * s : 8 * s + 8] for s in range(STRIPS)],
            extra_rows(new_means[g], counts[g]),
        )
        for s in range(SLOTS):
            out_ref[g * ROWS + 8 * s : g * ROWS + 8 * s + 8, :] = slots[s]


def solve_share(place, mine, theirs, means):
    smem = pl.BlockSpec(memory_space=pltpu.SMEM)
    vmem = pl.BlockSpec(memory_space=pltpu.VMEM)
    return pl.pallas_call(
        solve_kernel,
        in_specs=[smem, vmem, vmem, vmem],
        out_specs=vmem,
        out_shape=jax.ShapeDtypeStruct((GROUP * ROWS, WIDTH), F32),
        compiler_params=pltpu.CompilerParams(vmem_limit_bytes=VMEM_LIMIT),
        name="solve",
    )(place, mine, theirs, means)


def unpack_half(half, part_ref, factor_any, mean_ref, counts, buffer, sems):
    def copy_of(at):
        comp = half * HALF + at
        copy = pltpu.make_async_copy(buffer.at[at], factor_any.at[comp], sems.at[at])
        return comp < CLASSES * COMPS, copy

    def unpack(q, carry):
        for r in range(GROUP):
            at = q * GROUP + r
            comp = half * HALF + at
            slots = [part_ref[q, r * ROWS + 8 * s : r * ROWS + 8 * s + 8, :] for s in range(SLOTS)]
            strips = unpack_strips(slots)
            for s in range(STRIPS):
                buffer[at, 8 * s : 8 * s + 8, :] = strips[s]
            row, count = split_extra(slots[8])
            c = jnp.minimum(comp // COMPS, CLASSES)
            k = comp - comp // COMPS * COMPS
            mean_ref[k, pl.ds(c, 1), :] = row
            counts[k, pl.ds(c, 1), :] = count
        for r in range(GROUP):
            real, copy = copy_of(q * GROUP + r)
            pl.when(real)(copy.start)
        return carry

    def finish(at, carry):
        real, copy = copy_of(at)
        pl.when(real)(copy.wait)
        return carry

    lax.fori_loop(0, OWNERS, unpack, 0)
    return finish


def unpack_first_kernel(place, part_ref, factor_any, mean_ref, count_ref, buffer, sems):
    finish = unpack_half(place[0], part_ref, factor_any, mean_ref, count_ref, buffer, sems)
    lax.fori_loop(0, HALF, finish, 0)


def unpack_last_kernel(place, part_ref, begun_any, mean_part, count_part, factor_any, mean_ref, log_ref,
                       means, counts, buffer, sems):
    half = 1 - place[0]
    finish = unpack_half(half, part_ref, factor_any, means, counts, buffer, sems)
    comp = iota((PADDED, WIDTH), 0) * COMPS
    values = []
    for k in range(COMPS):
        here = (comp + k >= HALF) == (half == 1)
        mean_ref[k] = jnp.where(here, means[k], mean_part[k])[:CLASSES]
        values.append(jnp.where(here, counts[k], count_part[k])[:CLASSES])
    mask = iota((CLASSES, WIDTH), 0) == iota((CLASSES, WIDTH), 1)
    total = jnp.log(sum(values) + float(COMPS))
    for k in range(COMPS):
        logs = jnp.where(mask, jnp.log(values[k] + 1.0) - total, 0.0)
        log_ref[k : k + 1, :] = jnp.sum(logs, axis=0, keepdims=True)[:, :CLASSES]
    lax.fori_loop(0, HALF, finish, 0)


PADDED = 24


def unpack_all(place, here, there_of):
    vmem = pl.BlockSpec(memory_space=pltpu.VMEM)
    smem = pl.BlockSpec(memory_space=pltpu.SMEM)
    hbm = pl.BlockSpec(memory_space=pltpu.HBM)
    factor = jax.ShapeDtypeStruct((CLASSES * COMPS, WIDTH, WIDTH), F32)
    part = jax.ShapeDtypeStruct((COMPS, PADDED, WIDTH), F32)
    work = [pltpu.VMEM((HALF, WIDTH, WIDTH), F32), pltpu.SemaphoreType.DMA((HALF,))]
    rows = pltpu.VMEM(part.shape, F32)
    cost = pl.CostEstimate(flops=4000000, bytes_accessed=5000000, transcendentals=0)
    params = pltpu.CompilerParams(vmem_limit_bytes=VMEM_LIMIT)
    there = there_of(here)
    begun, mean_part, count_part = pl.pallas_call(
        unpack_first_kernel,
        in_specs=[smem, vmem],
        out_specs=[hbm, vmem, vmem],
        out_shape=[factor, part, part],
        scratch_shapes=work,
        compiler_params=params,
        cost_estimate=cost,
        name="unpack_first",
    )(place, here)
    return pl.pallas_call(
        unpack_last_kernel,
        in_specs=[smem, vmem, hbm, vmem, vmem],
        out_specs=[hbm, vmem, vmem],
        out_shape=[
            factor,
            jax.ShapeDtypeStruct((COMPS, CLASSES, WIDTH), F32),
            jax.ShapeDtypeStruct((COMPS, CLASSES), F32),
        ],
        input_output_aliases={2: 0},
        scratch_shapes=[rows, rows] + work,
        compiler_params=params,
        cost_estimate=cost,
        name="unpack_last",
    )(place, there, begun, mean_part, count_part)


def swap_cores(value):
    return lax.ppermute(value, "core", [(0, 1), (1, 0)])


def sum_far(value):
    total = value
    for hop in (2, 1, 3):
        total = total + lax.ppermute(value, "far", [(i, (i + hop) % 4) for i in range(4)])
    return total


def body(embeddings, class_blocks, class_counts, means, log_weights, factors):
    frames_here, pixels_here, width = embeddings.shape
    blocks = embeddings.reshape(frames_here * pixels_here // BLOCK, BLOCK, width)
    core = lax.axis_index("core").astype(jnp.int32)
    late = lax.axis_index("near").astype(jnp.int32)
    owner = (lax.axis_index("x") * 4 + lax.axis_index("y")).astype(jnp.int32)
    means_t = jnp.transpose(means, (1, 0, 2))
    place = core[None]
    own, other = local_moments(
        place, blocks, class_blocks[0, 0].T, class_counts[0, 0], log_weights.T, factors, means_t
    )
    peers = ("x", "y", "near")
    half = own + swap_cores(other)
    parts = lax.all_to_all(half.reshape(2 * OWNERS, PART, width), peers, 0, 0, tiled=True)
    mine = jnp.sum(parts, axis=0)
    mine = sum_far(mine)
    theirs = lax.ppermute(mine, "near", [(0, 1), (1, 0)])
    solved = solve_share(
        jnp.stack([core * HALF + owner * GROUP, late]), mine, theirs, means_t
    )
    spread = jnp.broadcast_to(solved[None], (OWNERS,) + solved.shape)
    here = lax.all_to_all(spread, ("x", "y"), 0, 0, tiled=True)
    new_factor, new_mean, new_log = unpack_all(place, here, swap_cores)
    return (
        new_log.T,
        jnp.transpose(new_mean, (1, 0, 2)),
        new_factor.reshape(CLASSES, COMPS, width, width),
    )


def solution(mesh):
    wide = Mesh(mesh.devices.reshape(4, 4, 2, 4, 2), ("x", "far", "near", "y", "core"))
    space = ("far", "near", "y", "core")
    return jax.shard_map(
        body,
        mesh=wide,
        in_specs=(P("x", space, None), P("x", space, None, None), P("x", space, None), P(), P(), P()),
        out_specs=(P(), P(), P()),
        check_vma=False,
    )
```

```python
import functools
import jax
import jax.numpy as jnp
from jax import lax
from jax.experimental import pallas as pl
from jax.experimental.pallas import tpu as pltpu
from jax.sharding import Mesh, PartitionSpec as P

CLASSES = 19
COMPS = 5
WIDTH = 128
BLOCK = 128
ROWS = 72
STRIPS = 16
F32 = jnp.float32
BF16 = jnp.bfloat16
SLOTS = 9
GROUP = 3
UNROLL = 3
OWNERS = 16
HALF = GROUP * OWNERS
SHARE = 224
PART = SHARE // 2
VMEM_LIMIT = 48 * 1024 * 1024


def iota(shape, axis):
    return lax.broadcasted_iota(jnp.int32, shape, axis)


def pieces(value, count):
    out = []
    for _ in range(count):
        part = value.astype(BF16)
        out.append(part)
        value = value - part.astype(F32)
    return out


def pack_strips(strips, extra):
    lane = iota((8, WIDTH), 1)
    out = [strips[0]]
    for s in range(1, 8):
        moved = pltpu.roll(strips[16 - s], 8 * s, 1)
        out.append(jnp.where(lane >= 8 * s, strips[s], moved))
    out.append(jnp.where(lane >= 64, strips[8], extra))
    return out


def unpack_strips(slots):
    lane = iota((8, WIDTH), 1)
    strips = [None] * 16
    strips[0] = slots[0]
    for s in range(1, 8):
        strips[s] = jnp.where(lane >= 8 * s, slots[s], 0.0)
        moved = pltpu.roll(slots[s], WIDTH - 8 * s, 1)
        strips[16 - s] = jnp.where(lane >= WIDTH - 8 * s, moved, 0.0)
    strips[8] = jnp.where(lane >= 64, slots[8], 0.0)
    return strips


def extra_rows(row, count):
    sub = iota((8, WIDTH), 0)
    later = pltpu.roll(jnp.broadcast_to(row, (8, WIDTH)), 64, 1)
    return jnp.where(sub == 0, row, jnp.where(sub == 1, later, jnp.where(sub == 2, count, 0.0)))


def split_extra(slot):
    lane = iota((8, WIDTH), 1)
    moved = pltpu.roll(slot, 64, 1)
    row = jnp.where(lane[0:1] < 64, slot[0:1], moved[1:2])
    count = jnp.where(lane[0:1] < 64, slot[2:3], moved[2:3])
    return row, count


def moments_kernel(place, lists_any, counts_any, lw_any, emb_any, fac_any, mean_any, own_ref, other_ref,
                   acc, tot, cnt, flipped, shift, const, rows_t, gate, items,
                   lists, list_counts, lw_ref, emb_ref, fac_ref, mean_ref, sems):
    pairs = ((lists_any, lists), (counts_any, list_counts), (lw_any, lw_ref), (emb_any, emb_ref),
             (fac_any, fac_ref), (mean_any, mean_ref))
    copies = [pltpu.make_async_copy(src, dst, sems.at[n]) for n, (src, dst) in enumerate(pairs)]
    for copy in copies:
        copy.start()
    sub = iota((8, WIDTH), 0)
    lane = iota((8, WIDTH), 1)
    ident = (iota((WIDTH, WIDTH), 0) == iota((WIDTH, WIDTH), 1)).astype(F32).astype(BF16)

    acc[...] = jnp.zeros_like(acc)
    tot[...] = jnp.zeros_like(tot)
    cnt[...] = jnp.zeros_like(cnt)

    copies[0].wait()
    copies[1].wait()

    def list_class(c, at):
        n = list_counts[c]

        def list_pair(t, at):
            items[0, at] = c
            items[1, at] = lists[2 * t, c]
            items[2, at] = lists[2 * t + 1, c]
            items[3, at] = jnp.where(2 * t + 1 < n, 2 * BLOCK, BLOCK)
            return at + 1

        return lax.fori_loop(0, (n + 1) // 2, list_pair, at)

    total_items = lax.fori_loop(0, CLASSES, list_class, jnp.int32(0))

    for copy in copies[2:]:
        copy.wait()

    def clamp(i):
        return jnp.minimum(jnp.maximum(i, 0), total_items - 1)

    def moments_of(i, u):
        at = clamp(i)
        c = items[0, at]
        rows = jnp.concatenate([emb_ref[items[1, at]], emb_ref[items[2, at]]], axis=0)
        weights = gate[u]
        flat = rows_t[u]
        both = jnp.concatenate([rows, rows], axis=0)
        for k in range(COMPS):
            high, low = pieces(flat * weights[k : k + 1], 2)
            acc[c * COMPS + k] += jnp.dot(
                jnp.concatenate([high, low], axis=1), both, preferred_element_type=F32
            )
        tall = jnp.concatenate([weights, jnp.zeros_like(weights)])
        sums = jnp.dot(jnp.concatenate(pieces(tall, 3)), rows, preferred_element_type=F32)
        tot[c] += sums[0:8] + sums[16:24] + sums[32:40]
        cnt[c] += weights[:, :BLOCK] + weights[:, BLOCK:]

    def scores_of(i, u):
        at = clamp(i)
        first = emb_ref[items[1, at]].astype(F32).T
        later = emb_ref[items[2, at]].astype(F32).T
        flat = jnp.concatenate([first, later], axis=1)
        square = jnp.zeros((8, 2 * BLOCK), F32)
        wide_sub = iota((8, 2 * BLOCK), 0)
        flat_half = flat.astype(BF16)
        offsets = shift[u].astype(BF16)
        row = iota((WIDTH, 2 * BLOCK), 0)
        for k in range(COMPS):
            ones = jnp.where((row >= 3 * k) & (row < 3 * k + 3), 1.0, 0.0).astype(BF16)
            centred = jnp.dot(
                jnp.concatenate([flipped[u, k], offsets], axis=1),
                jnp.concatenate([flat_half, ones], axis=0),
                preferred_element_type=F32,
            )
            line = jnp.sum(centred * centred, axis=0, keepdims=True)
            square = jnp.where(wide_sub == k, line, square)
        consts = const[u]
        scores = jnp.concatenate([consts, consts], axis=1) - 0.5 * square
        top = jnp.max(scores, axis=0, keepdims=True)
        weights = jnp.exp(scores - top)
        weights = weights / jnp.sum(weights, axis=0, keepdims=True)
        live = jnp.where((i >= 0) & (i < total_items), items[3, at], 0)
        gate[u] = jnp.where(iota((8, 2 * BLOCK), 1) < live, weights, 0.0)
        rows_t[u] = flat

    def prepare(i, u):
        c = items[0, clamp(i)]
        diag = jnp.ones((8, WIDTH), F32)
        prior = jnp.full((8, WIDTH), -1e30, F32)
        mean = mean_ref[:, c]
        mean_pieces = jnp.concatenate(
            pieces(jnp.concatenate([mean, jnp.zeros((16 - COMPS, WIDTH), F32)]), 3)
        )
        lines = []
        for k in range(COMPS):
            factor = fac_ref[c, k]
            wide = factor.astype(F32)
            on_diag = None
            for s in range(STRIPS):
                part = jnp.where(lane - 8 * s == sub, wide[8 * s : 8 * s + 8], 0.0)
                on_diag = part if on_diag is None else on_diag + part
            diag = jnp.where(sub == k, jnp.sum(on_diag, axis=0, keepdims=True), diag)
            prior = jnp.where(sub == k, lw_ref[k, c], prior)
            flipped[u, k] = wide.T.astype(BF16)
            parts = jnp.dot(mean_pieces, factor, preferred_element_type=F32)
            line = parts[k : k + 1] + parts[16 + k : 17 + k] + parts[32 + k : 33 + k]
            lines += [-p.astype(F32) for p in pieces(line, 3)]
        shift[u] = jnp.concatenate(lines + [jnp.zeros((WIDTH - 3 * COMPS, WIDTH), F32)], axis=0).T
        const[u] = jnp.sum(jnp.log(diag), axis=1, keepdims=True) + prior

    def stage(work, j):
        for u in range(UNROLL):
            work(UNROLL * j + u, u)

    def step(j, carry):
        stage(moments_of, j - 2)
        stage(scores_of, j - 1)
        stage(prepare, j)
        return carry

    groups = (total_items + UNROLL - 1) // UNROLL
    stage(prepare, 0)
    stage(scores_of, 0)
    stage(prepare, 1)
    lax.fori_loop(2, groups, step, 0)
    stage(moments_of, jnp.maximum(groups - 2, 0))
    stage(scores_of, groups - 1)
    stage(moments_of, groups - 1)

    def pack(q, carry):
        for base, out_ref in ((place[0], own_ref), (1 - place[0], other_ref)):
            for r in range(GROUP):
                slot = base * HALF + q * GROUP + r
                c = slot // COMPS
                k = slot - c * COMPS
                counted = cnt[c, pl.ds(k, 1), :]
                count = jnp.broadcast_to(jnp.sum(counted, axis=1, keepdims=True), (1, WIDTH))
                slots = pack_strips(
                    [acc[slot, 8 * s : 8 * s + 8, :] for s in range(STRIPS)],
                    extra_rows(tot[c, pl.ds(k, 1), :], count),
                )
                for s in range(SLOTS):
                    out_ref[q, r * ROWS + 8 * s : r * ROWS + 8 * s + 8, :] = slots[s]
            out_ref[q, GROUP * ROWS : SHARE, :] = jnp.zeros((SHARE - GROUP * ROWS, WIDTH), F32)
        return carry

    lax.fori_loop(0, OWNERS, pack, 0)


def local_moments(place, blocks, lists, list_counts, log_weights, factors, means):
    vmem = pl.BlockSpec(memory_space=pltpu.VMEM)
    smem = pl.BlockSpec(memory_space=pltpu.SMEM)
    anywhere = pl.BlockSpec(memory_space=pltpu.HBM)
    return pl.pallas_call(
        moments_kernel,
        in_specs=[smem] + [anywhere] * 6,
        out_specs=[vmem, vmem],
        scratch_shapes=[
            pltpu.VMEM(((CLASSES + 1) * COMPS, WIDTH, WIDTH), F32),
            pltpu.VMEM((CLASSES + 1, 8, WIDTH), F32),
            pltpu.VMEM((CLASSES + 1, 8, WIDTH), F32),
            pltpu.VMEM((UNROLL, COMPS, WIDTH, WIDTH), BF16),
            pltpu.VMEM((UNROLL, WIDTH, WIDTH), F32),
            pltpu.VMEM((UNROLL, 8, WIDTH), F32),
            pltpu.VMEM((UNROLL, WIDTH, 2 * BLOCK), F32),
            pltpu.VMEM((UNROLL, 8, 2 * BLOCK), F32),
            pltpu.SMEM((4, 128), jnp.int32),
            pltpu.SMEM(lists.shape, jnp.int32),
            pltpu.SMEM(list_counts.shape, jnp.int32),
            pltpu.SMEM(log_weights.shape, F32),
            pltpu.VMEM(blocks.shape, BF16),
            pltpu.VMEM(factors.shape, BF16),
            pltpu.VMEM(means.shape, F32),
            pltpu.SemaphoreType.DMA((6,)),
        ],
        out_shape=[jax.ShapeDtypeStruct((OWNERS, SHARE, WIDTH), F32)] * 2,
        compiler_params=pltpu.CompilerParams(vmem_limit_bytes=VMEM_LIMIT),
        name="moments",
    )(place, *[pltpu.with_memory_space_constraint(v, pltpu.HBM) for v in (lists, list_counts, log_weights, blocks, factors, means)])


def solve_kernel(place, mine_ref, theirs_ref, mean_ref, out_ref):
    lane = iota((8, WIDTH), 1)
    sub = iota((8, WIDTH), 0)
    early = place[1] == 0
    share = []
    for at in range(2):
        for t in range(PART // 8):
            cut = slice(8 * t, 8 * t + 8)
            share.append(jnp.where(early == (at == 0), mine_ref[cut, :], theirs_ref[cut, :]))
    strips, new_means, counts = [], [], []
    for g in range(GROUP):
        slots = share[SLOTS * g : SLOTS * g + SLOTS]
        totals, count = split_extra(slots[8])
        comp = jnp.minimum(place[0] + g, CLASSES * COMPS - 1)
        old = mean_ref[lax.rem(comp, COMPS), pl.ds(comp // COMPS, 1), :]
        denom = count + 1.0
        new = (totals + old) / denom
        old_t = jnp.broadcast_to(old, (WIDTH, WIDTH)).T
        new_t = jnp.broadcast_to(new * denom, (WIDTH, WIDTH)).T
        second = unpack_strips(slots)
        full = jnp.concatenate(second, axis=0)
        mirror = full.T
        rows = []
        for s in range(STRIPS):
            cut = slice(8 * s, 8 * s + 8)
            scatter = jnp.where(lane >= 8 * s, second[s], mirror[cut])
            scatter = scatter + old_t[cut] * old - new_t[cut] * new
            scatter = jnp.where(lane - 8 * s == sub, scatter + 1.0, scatter)
            rows.append(scatter / denom)
        strips.append(rows)
        new_means.append(new)
        counts.append(count)
    for s in range(STRIPS):
        for g in range(GROUP):
            rows = strips[g]
            block = (lane >= 8 * s) & (lane < 8 * s + 8)
            panel = rows[s]
            columns = [
                jnp.broadcast_to(panel[:, 8 * s + j : 8 * s + j + 1], (8, WIDTH)) for j in range(8)
            ]
            panel = jnp.where(block, jnp.where(lane - 8 * s == sub, 1.0, 0.0), panel)
            ahead = s + 1 < STRIPS
            if ahead:
                after = rows[s + 1]
                behind = [
                    jnp.broadcast_to(after[:, 8 * s + j : 8 * s + j + 1], (8, WIDTH))
                    for j in range(8)
                ]
                after = jnp.where(block, 0.0, after)
            pivots = jnp.ones((8, WIDTH), F32)
            for j in range(8):
                pivot = columns[j][j : j + 1]
                inverse = 1.0 / pivot
                pivots = jnp.where(sub == j, pivot, pivots)
                line = panel[j : j + 1]
                if ahead:
                    ratio = behind[j] * inverse
                    after = after - ratio * line
                    for l in range(j + 1, 8):
                        behind[l] = behind[l] - ratio * columns[l][j : j + 1]
                if j < 7:
                    ratio = jnp.where(sub > j, columns[j] * inverse, 0.0)
                    panel = panel - ratio * line
                    for l in range(j + 1, 8):
                        columns[l] = columns[l] - ratio * columns[l][j : j + 1]
            panel = panel * (1.0 / jnp.sqrt(pivots))
            rows[s] = panel
            if ahead:
                rows[s + 1] = after
            if s + 2 < STRIPS:
                a, b, d = [p.astype(F32) for p in pieces(panel, 3)]
                left = jnp.concatenate([a, a, b, b, a, d], axis=0).astype(BF16)
                right = jnp.concatenate([a, b, a, b, d, a], axis=0).astype(BF16)
                change = lax.dot_general(
                    left, right, (((0,), (0,)), ((), ())), preferred_element_type=F32
                )
                for t in range(s + 2, STRIPS):
                    base = jnp.where(block, 0.0, rows[t])
                    rows[t] = base - change[8 * t : 8 * t + 8]
    for g in range(GROUP):
        lower = jnp.concatenate(
            [jnp.where(lane - 8 * s <= sub, strips[g][s], 0.0) for s in range(STRIPS)], axis=0
        )
        upper = lower.T
        slots = pack_strips(
            [upper[8 * s : 8 * s + 8] for s in range(STRIPS)],
            extra_rows(new_means[g], counts[g]),
        )
        for s in range(SLOTS):
            out_ref[g * ROWS + 8 * s : g * ROWS + 8 * s + 8, :] = slots[s]


def solve_share(place, mine, theirs, means):
    smem = pl.BlockSpec(memory_space=pltpu.SMEM)
    vmem = pl.BlockSpec(memory_space=pltpu.VMEM)
    return pl.pallas_call(
        solve_kernel,
        in_specs=[smem, vmem, vmem, vmem],
        out_specs=vmem,
        out_shape=jax.ShapeDtypeStruct((GROUP * ROWS, WIDTH), F32),
        compiler_params=pltpu.CompilerParams(vmem_limit_bytes=VMEM_LIMIT),
        name="solve",
    )(place, mine, theirs, means)


def unpack_half(half, part_ref, factor_any, mean_ref, counts, buffer, sems):
    def copy_of(at):
        comp = half * HALF + at
        target = factor_any.at[jnp.minimum(comp, CLASSES * COMPS - 1)]
        copy = pltpu.make_async_copy(buffer.at[at], target, sems.at[at])
        return comp < CLASSES * COMPS, copy

    def unpack(q, carry):
        for r in range(GROUP):
            at = q * GROUP + r
            comp = half * HALF + at
            slots = [part_ref[q, r * ROWS + 8 * s : r * ROWS + 8 * s + 8, :] for s in range(SLOTS)]
            strips = unpack_strips(slots)
            for s in range(STRIPS):
                buffer[at, 8 * s : 8 * s + 8, :] = strips[s]
            row, count = split_extra(slots[8])
            c = jnp.minimum(comp // COMPS, CLASSES)
            k = comp - comp // COMPS * COMPS
            mean_ref[k, pl.ds(c, 1), :] = row
            counts[k, pl.ds(c, 1), :] = count
        for r in range(GROUP):
            real, copy = copy_of(q * GROUP + r)
            pl.when(real)(copy.start)
        return carry

    def finish(at, carry):
        real, copy = copy_of(at)
        pl.when(real)(copy.wait)
        return carry

    lax.fori_loop(0, OWNERS, unpack, 0)
    return finish


def unpack_first_kernel(place, part_ref, factor_any, mean_ref, count_ref, buffer, sems):
    finish = unpack_half(place[0], part_ref, factor_any, mean_ref, count_ref, buffer, sems)
    lax.fori_loop(0, HALF, finish, 0)


def unpack_last_kernel(place, part_ref, begun_any, mean_part, count_part, factor_any, mean_ref, log_ref,
                       means, counts, buffer, sems):
    half = 1 - place[0]
    finish = unpack_half(half, part_ref, factor_any, means, counts, buffer, sems)
    comp = iota((PADDED, WIDTH), 0) * COMPS
    values = []
    for k in range(COMPS):
        here = (comp + k >= HALF) == (half == 1)
        mean_ref[k] = jnp.where(here, means[k], mean_part[k])[:CLASSES]
        values.append(jnp.where(here, counts[k], count_part[k])[:CLASSES])
    mask = iota((CLASSES, WIDTH), 0) == iota((CLASSES, WIDTH), 1)
    total = jnp.log(sum(values) + float(COMPS))
    for k in range(COMPS):
        logs = jnp.where(mask, jnp.log(values[k] + 1.0) - total, 0.0)
        log_ref[k : k + 1, :] = jnp.sum(logs, axis=0, keepdims=True)[:, :CLASSES]
    lax.fori_loop(0, HALF, finish, 0)


PADDED = 24


def unpack_all(place, here, there_of):
    vmem = pl.BlockSpec(memory_space=pltpu.VMEM)
    smem = pl.BlockSpec(memory_space=pltpu.SMEM)
    hbm = pl.BlockSpec(memory_space=pltpu.HBM)
    factor = jax.ShapeDtypeStruct((CLASSES * COMPS, WIDTH, WIDTH), F32)
    part = jax.ShapeDtypeStruct((COMPS, PADDED, WIDTH), F32)
    work = [pltpu.VMEM((HALF, WIDTH, WIDTH), F32), pltpu.SemaphoreType.DMA((HALF,))]
    rows = pltpu.VMEM(part.shape, F32)
    cost = pl.CostEstimate(flops=4000000, bytes_accessed=5000000, transcendentals=0)
    params = pltpu.CompilerParams(vmem_limit_bytes=VMEM_LIMIT)
    there = there_of(here)
    begun, mean_part, count_part = pl.pallas_call(
        unpack_first_kernel,
        in_specs=[smem, vmem],
        out_specs=[hbm, vmem, vmem],
        out_shape=[factor, part, part],
        scratch_shapes=work,
        compiler_params=params,
        cost_estimate=cost,
        name="unpack_first",
    )(place, here)
    return pl.pallas_call(
        unpack_last_kernel,
        in_specs=[smem, vmem, hbm, vmem, vmem],
        out_specs=[hbm, vmem, vmem],
        out_shape=[
            factor,
            jax.ShapeDtypeStruct((COMPS, CLASSES, WIDTH), F32),
            jax.ShapeDtypeStruct((COMPS, CLASSES), F32),
        ],
        input_output_aliases={2: 0},
        scratch_shapes=[rows, rows] + work,
        compiler_params=params,
        cost_estimate=cost,
        name="unpack_last",
    )(place, there, begun, mean_part, count_part)


def swap_cores(value):
    return lax.ppermute(value, "core", [(0, 1), (1, 0)])


def sum_far(value):
    total = value
    for hop in (2, 1, 3):
        total = total + lax.ppermute(value, "far", [(i, (i + hop) % 4) for i in range(4)])
    return total


def body(embeddings, class_blocks, class_counts, means, log_weights, factors):
    frames_here, pixels_here, width = embeddings.shape
    blocks = embeddings.reshape(frames_here * pixels_here // BLOCK, BLOCK, width)
    core = lax.axis_index("core").astype(jnp.int32)
    late = lax.axis_index("near").astype(jnp.int32)
    owner = (lax.axis_index("x") * 4 + lax.axis_index("y")).astype(jnp.int32)
    means_t = jnp.transpose(means, (1, 0, 2))
    place = core[None]
    own, other = local_moments(
        place, blocks, class_blocks[0, 0].T, class_counts[0, 0], log_weights.T, factors, means_t
    )
    peers = ("x", "y", "near")
    half = own + swap_cores(other)
    parts = lax.all_to_all(half.reshape(2 * OWNERS, PART, width), peers, 0, 0, tiled=True)
    mine = jnp.sum(parts, axis=0)
    mine = sum_far(mine)
    theirs = lax.ppermute(mine, "near", [(0, 1), (1, 0)])
    solved = solve_share(
        jnp.stack([core * HALF + owner * GROUP, late]), mine, theirs, means_t
    )
    spread = jnp.broadcast_to(solved[None], (OWNERS,) + solved.shape)
    here = lax.all_to_all(spread, ("x", "y"), 0, 0, tiled=True)
    new_factor, new_mean, new_log = unpack_all(place, here, swap_cores)
    return (
        new_log.T,
        jnp.transpose(new_mean, (1, 0, 2)),
        new_factor.reshape(CLASSES, COMPS, width, width),
    )


def solution(mesh):
    wide = Mesh(mesh.devices.reshape(4, 4, 2, 4, 2), ("x", "far", "near", "y", "core"))
    space = ("far", "near", "y", "core")
    return jax.shard_map(
        body,
        mesh=wide,
        in_specs=(P("x", space, None), P("x", space, None, None), P("x", space, None), P(), P(), P()),
        out_specs=(P(), P(), P()),
        check_vma=False,
    )
```

```python
import functools
import jax
import jax.numpy as jnp
from jax import lax
from jax.experimental import pallas as pl
from jax.experimental.pallas import tpu as pltpu
from jax.sharding import Mesh, PartitionSpec as P

CLASSES = 19
COMPS = 5
WIDTH = 128
BLOCK = 128
ROWS = 72
STRIPS = 16
F32 = jnp.float32
BF16 = jnp.bfloat16
SLOTS = 9
GROUP = 3
UNROLL = 3
OWNERS = 16
HALF = GROUP * OWNERS
SHARE = 224
PART = SHARE // 2
VMEM_LIMIT = 48 * 1024 * 1024


def iota(shape, axis):
    return lax.broadcasted_iota(jnp.int32, shape, axis)


def pieces(value, count):
    out = []
    for _ in range(count):
        part = value.astype(BF16)
        out.append(part)
        value = value - part.astype(F32)
    return out


def pack_strips(strips, extra):
    lane = iota((8, WIDTH), 1)
    out = [strips[0]]
    for s in range(1, 8):
        moved = pltpu.roll(strips[16 - s], 8 * s, 1)
        out.append(jnp.where(lane >= 8 * s, strips[s], moved))
    out.append(jnp.where(lane >= 64, strips[8], extra))
    return out


def unpack_strips(slots):
    lane = iota((8, WIDTH), 1)
    strips = [None] * 16
    strips[0] = slots[0]
    for s in range(1, 8):
        strips[s] = jnp.where(lane >= 8 * s, slots[s], 0.0)
        moved = pltpu.roll(slots[s], WIDTH - 8 * s, 1)
        strips[16 - s] = jnp.where(lane >= WIDTH - 8 * s, moved, 0.0)
    strips[8] = jnp.where(lane >= 64, slots[8], 0.0)
    return strips


def extra_rows(row, count):
    sub = iota((8, WIDTH), 0)
    later = pltpu.roll(jnp.broadcast_to(row, (8, WIDTH)), 64, 1)
    return jnp.where(sub == 0, row, jnp.where(sub == 1, later, jnp.where(sub == 2, count, 0.0)))


def split_extra(slot):
    lane = iota((8, WIDTH), 1)
    moved = pltpu.roll(slot, 64, 1)
    row = jnp.where(lane[0:1] < 64, slot[0:1], moved[1:2])
    count = jnp.where(lane[0:1] < 64, slot[2:3], moved[2:3])
    return row, count


def moments_kernel(place, lists_any, counts_any, lw_any, emb_any, fac_any, mean_any, own_ref, other_ref,
                   acc, tot, cnt, flipped, shift, const, rows_t, gate, items,
                   lists, list_counts, lw_ref, emb_ref, fac_ref, mean_ref, sems):
    pairs = ((lists_any, lists), (counts_any, list_counts), (lw_any, lw_ref), (emb_any, emb_ref),
             (fac_any, fac_ref), (mean_any, mean_ref))
    copies = [pltpu.make_async_copy(src, dst, sems.at[n]) for n, (src, dst) in enumerate(pairs)]
    for copy in copies:
        copy.start()
    sub = iota((8, WIDTH), 0)
    lane = iota((8, WIDTH), 1)
    ident = (iota((WIDTH, WIDTH), 0) == iota((WIDTH, WIDTH), 1)).astype(F32).astype(BF16)

    acc[...] = jnp.zeros_like(acc)
    tot[...] = jnp.zeros_like(tot)
    cnt[...] = jnp.zeros_like(cnt)

    copies[0].wait()
    copies[1].wait()

    def list_class(c, at):
        n = list_counts[c]

        def list_pair(t, at):
            items[0, at] = c
            items[1, at] = lists[2 * t, c]
            items[2, at] = lists[2 * t + 1, c]
            items[3, at] = jnp.where(2 * t + 1 < n, 2 * BLOCK, BLOCK)
            return at + 1

        return lax.fori_loop(0, (n + 1) // 2, list_pair, at)

    total_items = lax.fori_loop(0, CLASSES, list_class, jnp.int32(0))

    for copy in copies[2:]:
        copy.wait()

    def clamp(i):
        return jnp.minimum(jnp.maximum(i, 0), total_items - 1)

    def moments_of(i, u):
        at = clamp(i)
        c = items[0, at]
        rows = jnp.concatenate([emb_ref[items[1, at]], emb_ref[items[2, at]]], axis=0)
        weights = gate[u]
        flat = rows_t[u]
        both = jnp.concatenate([rows, rows], axis=0)
        for k in range(COMPS):
            high, low = pieces(flat * weights[k : k + 1], 2)
            acc[c * COMPS + k] += jnp.dot(
                jnp.concatenate([high, low], axis=1), both, preferred_element_type=F32
            )
        tall = jnp.concatenate([weights, jnp.zeros_like(weights)])
        sums = jnp.dot(jnp.concatenate(pieces(tall, 3)), rows, preferred_element_type=F32)
        tot[c] += sums[0:8] + sums[16:24] + sums[32:40]
        cnt[c] += weights[:, :BLOCK] + weights[:, BLOCK:]

    def scores_of(i, u):
        at = clamp(i)
        first = emb_ref[items[1, at]].astype(F32).T
        later = emb_ref[items[2, at]].astype(F32).T
        flat = jnp.concatenate([first, later], axis=1)
        square = jnp.zeros((8, 2 * BLOCK), F32)
        wide_sub = iota((8, 2 * BLOCK), 0)
        flat_half = flat.astype(BF16)
        offsets = shift[u].astype(BF16)
        row = iota((WIDTH, 2 * BLOCK), 0)
        for k in range(COMPS):
            ones = jnp.where((row >= 3 * k) & (row < 3 * k + 3), 1.0, 0.0).astype(BF16)
            centred = jnp.dot(
                jnp.concatenate([flipped[u, k], offsets], axis=1),
                jnp.concatenate([flat_half, ones], axis=0),
                preferred_element_type=F32,
            )
            line = jnp.sum(centred * centred, axis=0, keepdims=True)
            square = jnp.where(wide_sub == k, line, square)
        consts = const[u]
        scores = jnp.concatenate([consts, consts], axis=1) - 0.5 * square
        top = jnp.max(scores, axis=0, keepdims=True)
        weights = jnp.exp(scores - top)
        weights = weights / jnp.sum(weights, axis=0, keepdims=True)
        live = jnp.where((i >= 0) & (i < total_items), items[3, at], 0)
        gate[u] = jnp.where(iota((8, 2 * BLOCK), 1) < live, weights, 0.0)
        rows_t[u] = flat

    def prepare(i, u):
        c = items[0, clamp(i)]
        diag = jnp.ones((8, WIDTH), F32)
        prior = jnp.full((8, WIDTH), -1e30, F32)
        mean = mean_ref[:, c]
        mean_pieces = jnp.concatenate(
            pieces(jnp.concatenate([mean, jnp.zeros((16 - COMPS, WIDTH), F32)]), 3)
        )
        lines = []
        for k in range(COMPS):
            factor = fac_ref[c, k]
            wide = factor.astype(F32)
            on_diag = None
            for s in range(STRIPS):
                part = jnp.where(lane - 8 * s == sub, wide[8 * s : 8 * s + 8], 0.0)
                on_diag = part if on_diag is None else on_diag + part
            diag = jnp.where(sub == k, jnp.sum(on_diag, axis=0, keepdims=True), diag)
            prior = jnp.where(sub == k, lw_ref[k, c], prior)
            flipped[u, k] = wide.T.astype(BF16)
            parts = jnp.dot(mean_pieces, factor, preferred_element_type=F32)
            line = parts[k : k + 1] + parts[16 + k : 17 + k] + parts[32 + k : 33 + k]
            lines += [-p.astype(F32) for p in pieces(line, 3)]
        shift[u] = jnp.concatenate(lines + [jnp.zeros((WIDTH - 3 * COMPS, WIDTH), F32)], axis=0).T
        const[u] = jnp.sum(jnp.log(diag), axis=1, keepdims=True) + prior

    def stage(work, j):
        for u in range(UNROLL):
            work(UNROLL * j + u, u)

    def step(j, carry):
        stage(moments_of, j - 2)
        stage(scores_of, j - 1)
        stage(prepare, j)
        return carry

    groups = (total_items + UNROLL - 1) // UNROLL
    stage(prepare, 0)
    stage(scores_of, 0)
    stage(prepare, 1)
    lax.fori_loop(2, groups, step, 0)
    stage(moments_of, jnp.maximum(groups - 2, 0))
    stage(scores_of, groups - 1)
    stage(moments_of, groups - 1)

    def pack(q, carry):
        for base, out_ref in ((place[0], own_ref), (1 - place[0], other_ref)):
            for r in range(GROUP):
                slot = base * HALF + q * GROUP + r
                c = slot // COMPS
                k = slot - c * COMPS
                counted = cnt[c, pl.ds(k, 1), :]
                count = jnp.broadcast_to(jnp.sum(counted, axis=1, keepdims=True), (1, WIDTH))
                slots = pack_strips(
                    [acc[slot, 8 * s : 8 * s + 8, :] for s in range(STRIPS)],
                    extra_rows(tot[c, pl.ds(k, 1), :], count),
                )
                for s in range(SLOTS):
                    out_ref[q, r * ROWS + 8 * s : r * ROWS + 8 * s + 8, :] = slots[s]
            out_ref[q, GROUP * ROWS : SHARE, :] = jnp.zeros((SHARE - GROUP * ROWS, WIDTH), F32)
        return carry

    lax.fori_loop(0, OWNERS, pack, 0)


def local_moments(place, blocks, lists, list_counts, log_weights, factors, means):
    vmem = pl.BlockSpec(memory_space=pltpu.VMEM)
    smem = pl.BlockSpec(memory_space=pltpu.SMEM)
    anywhere = pl.BlockSpec(memory_space=pltpu.HBM)
    return pl.pallas_call(
        moments_kernel,
        in_specs=[smem] + [anywhere] * 6,
        out_specs=[vmem, vmem],
        scratch_shapes=[
            pltpu.VMEM(((CLASSES + 1) * COMPS, WIDTH, WIDTH), F32),
            pltpu.VMEM((CLASSES + 1, 8, WIDTH), F32),
            pltpu.VMEM((CLASSES + 1, 8, WIDTH), F32),
            pltpu.VMEM((UNROLL, COMPS, WIDTH, WIDTH), BF16),
            pltpu.VMEM((UNROLL, WIDTH, WIDTH), F32),
            pltpu.VMEM((UNROLL, 8, WIDTH), F32),
            pltpu.VMEM((UNROLL, WIDTH, 2 * BLOCK), F32),
            pltpu.VMEM((UNROLL, 8, 2 * BLOCK), F32),
            pltpu.SMEM((4, 128), jnp.int32),
            pltpu.SMEM(lists.shape, jnp.int32),
            pltpu.SMEM(list_counts.shape, jnp.int32),
            pltpu.SMEM(log_weights.shape, F32),
            pltpu.VMEM(blocks.shape, BF16),
            pltpu.VMEM(factors.shape, BF16),
            pltpu.VMEM(means.shape, F32),
            pltpu.SemaphoreType.DMA((6,)),
        ],
        out_shape=[jax.ShapeDtypeStruct((OWNERS, SHARE, WIDTH), F32)] * 2,
        compiler_params=pltpu.CompilerParams(vmem_limit_bytes=VMEM_LIMIT),
        name="moments",
    )(place, *[pltpu.with_memory_space_constraint(v, pltpu.HBM) for v in (lists, list_counts, log_weights, blocks, factors, means)])


def solve_kernel(place, mine_ref, theirs_ref, mean_ref, out_ref):
    lane = iota((8, WIDTH), 1)
    sub = iota((8, WIDTH), 0)
    early = place[1] == 0
    share = []
    for at in range(2):
        for t in range(PART // 8):
            cut = slice(8 * t, 8 * t + 8)
            share.append(jnp.where(early == (at == 0), mine_ref[cut, :], theirs_ref[cut, :]))
    strips, new_means, counts = [], [], []
    for g in range(GROUP):
        slots = share[SLOTS * g : SLOTS * g + SLOTS]
        totals, count = split_extra(slots[8])
        comp = jnp.minimum(place[0] + g, CLASSES * COMPS - 1)
        old = mean_ref[lax.rem(comp, COMPS), pl.ds(comp // COMPS, 1), :]
        denom = count + 1.0
        new = (totals + old) / denom
        old_t = jnp.broadcast_to(old, (WIDTH, WIDTH)).T
        new_t = jnp.broadcast_to(new * denom, (WIDTH, WIDTH)).T
        second = unpack_strips(slots)
        full = jnp.concatenate(second, axis=0)
        mirror = full.T
        rows = []
        for s in range(STRIPS):
            cut = slice(8 * s, 8 * s + 8)
            scatter = jnp.where(lane >= 8 * s, second[s], mirror[cut])
            scatter = scatter + old_t[cut] * old - new_t[cut] * new
            scatter = jnp.where(lane - 8 * s == sub, scatter + 1.0, scatter)
            rows.append(scatter / denom)
        strips.append(rows)
        new_means.append(new)
        counts.append(count)
    for s in range(STRIPS):
        for g in range(GROUP):
            rows = strips[g]
            block = (lane >= 8 * s) & (lane < 8 * s + 8)
            panel = rows[s]
            columns = [
                jnp.broadcast_to(panel[:, 8 * s + j : 8 * s + j + 1], (8, WIDTH)) for j in range(8)
            ]
            panel = jnp.where(block, jnp.where(lane - 8 * s == sub, 1.0, 0.0), panel)
            ahead = s + 1 < STRIPS
            if ahead:
                after = rows[s + 1]
                behind = [
                    jnp.broadcast_to(after[:, 8 * s + j : 8 * s + j + 1], (8, WIDTH))
                    for j in range(8)
                ]
                after = jnp.where(block, 0.0, after)
            pivots = jnp.ones((8, WIDTH), F32)
            for j in range(8):
                pivot = columns[j][j : j + 1]
                inverse = 1.0 / pivot
                pivots = jnp.where(sub == j, pivot, pivots)
                line = panel[j : j + 1]
                if ahead:
                    ratio = behind[j] * inverse
                    after = after - ratio * line
                    for l in range(j + 1, 8):
                        behind[l] = behind[l] - ratio * columns[l][j : j + 1]
                if j < 7:
                    ratio = jnp.where(sub > j, columns[j] * inverse, 0.0)
                    panel = panel - ratio * line
                    for l in range(j + 1, 8):
                        columns[l] = columns[l] - ratio * columns[l][j : j + 1]
            panel = panel * (1.0 / jnp.sqrt(pivots))
            rows[s] = panel
            if ahead:
                rows[s + 1] = after
            if s + 2 < STRIPS:
                a, b, d = [p.astype(F32) for p in pieces(panel, 3)]
                left = jnp.concatenate([a, a, b, b, a, d], axis=0).astype(BF16)
                right = jnp.concatenate([a, b, a, b, d, a], axis=0).astype(BF16)
                change = lax.dot_general(
                    left, right, (((0,), (0,)), ((), ())), preferred_element_type=F32
                )
                for t in range(s + 2, STRIPS):
                    base = jnp.where(block, 0.0, rows[t])
                    rows[t] = base - change[8 * t : 8 * t + 8]
    for g in range(GROUP):
        lower = jnp.concatenate(
            [jnp.where(lane - 8 * s <= sub, strips[g][s], 0.0) for s in range(STRIPS)], axis=0
        )
        upper = lower.T
        slots = pack_strips(
            [upper[8 * s : 8 * s + 8] for s in range(STRIPS)],
            extra_rows(new_means[g], counts[g]),
        )
        for s in range(SLOTS):
            out_ref[g * ROWS + 8 * s : g * ROWS + 8 * s + 8, :] = slots[s]


def solve_share(place, mine, theirs, means):
    smem = pl.BlockSpec(memory_space=pltpu.SMEM)
    vmem = pl.BlockSpec(memory_space=pltpu.VMEM)
    return pl.pallas_call(
        solve_kernel,
        in_specs=[smem, vmem, vmem, vmem],
        out_specs=vmem,
        out_shape=jax.ShapeDtypeStruct((GROUP * ROWS, WIDTH), F32),
        compiler_params=pltpu.CompilerParams(vmem_limit_bytes=VMEM_LIMIT),
        name="solve",
    )(place, mine, theirs, means)


def unpack_half(half, part_ref, factor_any, mean_ref, counts, buffer, sems):
    def copy_of(at):
        comp = half * HALF + at
        target = factor_any.at[jnp.minimum(comp, CLASSES * COMPS - 1)]
        copy = pltpu.make_async_copy(buffer.at[at], target, sems.at[at])
        return comp < CLASSES * COMPS, copy

    def unpack(q, carry):
        for r in range(GROUP):
            at = q * GROUP + r
            comp = half * HALF + at
            slots = [part_ref[q, r * ROWS + 8 * s : r * ROWS + 8 * s + 8, :] for s in range(SLOTS)]
            strips = unpack_strips(slots)
            for s in range(STRIPS):
                buffer[at, 8 * s : 8 * s + 8, :] = strips[s]
            row, count = split_extra(slots[8])
            c = jnp.minimum(comp // COMPS, CLASSES)
            k = comp - comp // COMPS * COMPS
            mean_ref[k, pl.ds(c, 1), :] = row
            counts[k, pl.ds(c, 1), :] = count
        for r in range(GROUP):
            real, copy = copy_of(q * GROUP + r)
            pl.when(real)(copy.start)
        return carry

    def finish(at, carry):
        real, copy = copy_of(at)
        pl.when(real)(copy.wait)
        return carry

    lax.fori_loop(0, OWNERS, unpack, 0)
    return finish


def unpack_first_kernel(place, part_ref, factor_any, mean_ref, count_ref, buffer, sems):
    finish = unpack_half(place[0], part_ref, factor_any, mean_ref, count_ref, buffer, sems)
    lax.fori_loop(0, HALF, finish, 0)


def unpack_last_kernel(place, part_ref, begun_any, mean_part, count_part, factor_any, mean_ref, log_ref,
                       means, counts, buffer, sems):
    half = 1 - place[0]
    finish = unpack_half(half, part_ref, factor_any, means, counts, buffer, sems)
    comp = iota((PADDED, WIDTH), 0) * COMPS
    values = []
    for k in range(COMPS):
        here = (comp + k >= HALF) == (half == 1)
        mean_ref[k] = jnp.where(here, means[k], mean_part[k])[:CLASSES]
        values.append(jnp.where(here, counts[k], count_part[k])[:CLASSES])
    mask = iota((CLASSES, WIDTH), 0) == iota((CLASSES, WIDTH), 1)
    total = jnp.log(sum(values) + float(COMPS))
    for k in range(COMPS):
        logs = jnp.where(mask, jnp.log(values[k] + 1.0) - total, 0.0)
        log_ref[k : k + 1, :] = jnp.sum(logs, axis=0, keepdims=True)[:, :CLASSES]
    lax.fori_loop(0, HALF, finish, 0)


PADDED = 24


def unpack_all(place, here, there_of):
    vmem = pl.BlockSpec(memory_space=pltpu.VMEM)
    smem = pl.BlockSpec(memory_space=pltpu.SMEM)
    hbm = pl.BlockSpec(memory_space=pltpu.HBM)
    factor = jax.ShapeDtypeStruct((CLASSES * COMPS, WIDTH, WIDTH), F32)
    part = jax.ShapeDtypeStruct((COMPS, PADDED, WIDTH), F32)
    work = [pltpu.VMEM((HALF, WIDTH, WIDTH), F32), pltpu.SemaphoreType.DMA((HALF,))]
    rows = pltpu.VMEM(part.shape, F32)
    cost = pl.CostEstimate(flops=4000000, bytes_accessed=5000000, transcendentals=0)
    params = pltpu.CompilerParams(vmem_limit_bytes=VMEM_LIMIT)
    there = there_of(here)
    begun, mean_part, count_part = pl.pallas_call(
        unpack_first_kernel,
        in_specs=[smem, vmem],
        out_specs=[hbm, vmem, vmem],
        out_shape=[factor, part, part],
        scratch_shapes=work,
        compiler_params=params,
        cost_estimate=cost,
        name="unpack_first",
    )(place, here)
    return pl.pallas_call(
        unpack_last_kernel,
        in_specs=[smem, vmem, hbm, vmem, vmem],
        out_specs=[hbm, vmem, vmem],
        out_shape=[
            factor,
            jax.ShapeDtypeStruct((COMPS, CLASSES, WIDTH), F32),
            jax.ShapeDtypeStruct((COMPS, CLASSES), F32),
        ],
        input_output_aliases={2: 0},
        scratch_shapes=[rows, rows] + work,
        compiler_params=params,
        cost_estimate=cost,
        name="unpack_last",
    )(place, there, begun, mean_part, count_part)


def swap_cores(value):
    return lax.ppermute(value, "core", [(0, 1), (1, 0)])


def sum_far(value):
    total = value
    for partners in ((1, 0, 3, 2), (3, 2, 1, 0)):
        total = total + lax.ppermute(total, "far", list(enumerate(partners)))
    return total


def body(embeddings, class_blocks, class_counts, means, log_weights, factors):
    frames_here, pixels_here, width = embeddings.shape
    blocks = embeddings.reshape(frames_here * pixels_here // BLOCK, BLOCK, width)
    core = lax.axis_index("core").astype(jnp.int32)
    late = lax.axis_index("near").astype(jnp.int32)
    owner = (lax.axis_index("x") * 4 + lax.axis_index("y")).astype(jnp.int32)
    means_t = jnp.transpose(means, (1, 0, 2))
    place = core[None]
    own, other = local_moments(
        place, blocks, class_blocks[0, 0].T, class_counts[0, 0], log_weights.T, factors, means_t
    )
    peers = ("x", "y", "near")
    half = own + swap_cores(other)
    parts = lax.all_to_all(half.reshape(2 * OWNERS, PART, width), peers, 0, 0, tiled=True)
    mine = jnp.sum(parts, axis=0)
    mine = sum_far(mine)
    theirs = lax.ppermute(mine, "near", [(0, 1), (1, 0)])
    solved = solve_share(
        jnp.stack([core * HALF + owner * GROUP, late]), mine, theirs, means_t
    )
    spread = jnp.broadcast_to(solved[None], (OWNERS,) + solved.shape)
    here = lax.all_to_all(spread, ("x", "y"), 0, 0, tiled=True)
    new_factor, new_mean, new_log = unpack_all(place, here, swap_cores)
    return (
        new_log.T,
        jnp.transpose(new_mean, (1, 0, 2)),
        new_factor.reshape(CLASSES, COMPS, width, width),
    )


def solution(mesh):
    wide = Mesh(mesh.devices.reshape(4, 4, 2, 4, 2), ("x", "far", "near", "y", "core"))
    space = ("far", "near", "y", "core")
    return jax.shard_map(
        body,
        mesh=wide,
        in_specs=(P("x", space, None), P("x", space, None, None), P("x", space, None), P(), P(), P()),
        out_specs=(P(), P(), P()),
        check_vma=False,
    )
```
